128 devices in a mesh: section: 8 (over x, core), ep: 16 (over y, z).
Axes of the slice: x: 4, y: 4, z: 4, core: 2. Of those that a mesh axis runs over, the one named last changes fastest.
Arguments:
- upstream: bfloat16 [8, 2048, 7168], P('section', 'ep'), may hold values from -6 to 6
- routes: int32 [8, 2048, 2], P('section', 'ep'), may hold values from 0 to 3, all different within a row; in each aligned block of 128 rows (0 to 127, 128 to 255, ..., all dimensions but the last counted through in order) at most 80 rows name the same one
- combine_weights: bfloat16 [8, 2048, 2], P('section', 'ep'), may hold values from 0.049804688 to 1
- gate_saved: bfloat16 [8, 16, 80, 4096], P('section', None, None, 'ep'), may hold values from -3 to 3
- up_saved: bfloat16 [8, 16, 80, 4096], P('section', None, None, 'ep'), may hold values from -3 to 3
- w_gate: bfloat16 [8, 7168, 4096], P('section', None, 'ep'), may hold values from -0.0625 to 0.0625
- w_up: bfloat16 [8, 7168, 4096], P('section', None, 'ep'), may hold values from -0.0625 to 0.0625
- w_down: bfloat16 [8, 4096, 7168], P('section', 'ep'), may hold values from -0.1875 to 0.1875
Outputs:
- grad_input: bfloat16 [8, 2048, 7168], P('section', 'ep')
- router_grad: float32 [8, 2048, 2], P('section', 'ep')
The draws below stay inside these ranges and needn't reach their ends.
Inputs may be any that keep to these rules, and one draw needn't show every extreme that they name: `routes`: within the 128 tokens of one device (aligned blocks), no expert is named by more than 80 route entries, a bound that some block reaches; a token names 2 different experts.
All inputs are finite; a program needn't handle non-finite values.
Results may differ from the reference program's by a relative error of at most 0.005.
Values may be sent and summed in bfloat16 or wider, within the bound.
A program may use at most 192 MiB of HBM per device.

```python
import math
from functools import partial
import jax
import jax.numpy as jnp
import numpy as np

D = 7168
FF = 1024
E_WIN = 4
TOPK = 2
TOK_DEV = 128
TOKENS = 2048
CAP = 80
N_SECTION = 8
N_EP = 16


def block_scale(stream_key, extent, cuts, smallest, high):
    def one(dim, blocks):
        heights = jax.random.uniform(jax.random.fold_in(jax.random.fold_in(stream_key, 6), dim), (blocks,), jnp.float32, smallest / len(cuts), high / len(cuts))
        return jnp.repeat(jnp.exp(heights), extent[dim] // blocks).reshape((-1,) + (1,) * (len(extent) - dim - 1))

    factor_of = one(*cuts[0])
    for cut in cuts[1:]:
        factor_of = factor_of * one(*cut)
    return factor_of


def deal_out(own_key, own, number, rows, number_of, top, limit, slope):
    ranking = jax.random.permutation(own_key, number_of)
    heavy_load, ordinary = portions_of(number_of, rows * top, limit, slope, True), portions_of(number_of, rows * top, limit, slope, False)
    places = jnp.arange(number_of)

    def named(tallies, turn):
        used = int((tallies > 0).sum())
        fixed = max(1, used // 4)
        passed = fixed + (places - fixed + turn * (used - fixed)) % max(1, number_of - fixed)
        return jnp.zeros((number_of,), jnp.int32).at[ranking[jnp.where(places < fixed, places, passed)]].set(jnp.asarray(tallies, jnp.int32))

    tallies = jnp.where(number % 4 == 0, named(heavy_load, number // 4), named(ordinary, number - number // 4 - 1))
    mixed = jax.random.permutation(jax.random.fold_in(own, 3), number_of)
    giver, taker = mixed[0:number_of // 2 * 2:2], mixed[1:number_of // 2 * 2:2]
    slack = jnp.minimum(tallies[giver] - 1, limit - tallies[taker]) // 2
    slack = jnp.where((giver == ranking[0]) | (taker == ranking[0]) | (tallies[taker] == 0), 0, jnp.maximum(slack, 0))
    passed = jax.random.randint(jax.random.fold_in(own, 4), (number_of // 2,), 0, 1 << 20) % (slack + 1)
    tallies = tallies.at[giver].add(-passed).at[taker].add(passed)
    labels = jnp.searchsorted(jnp.cumsum(tallies), jnp.arange(rows * top), side="right").astype(jnp.int32)
    listing = labels.reshape(top, rows).T
    listing = listing[jax.random.permutation(jax.random.fold_in(own, 1), rows)]
    turn = jax.random.randint(jax.random.fold_in(own, 2), (rows, 1), 0, top)
    return jnp.take_along_axis(listing, (jnp.arange(top)[None, :] + turn) % top, axis=1)


def portions_of(amount, total, limit, lean, full):
    portions = [(1 << 20) // math.isqrt(standing ** lean) + 1 for standing in range(1, amount + 1)]
    largest = limit if full else min(limit, max(-(-total // amount), total * portions[0] // sum(portions)))
    least = 1 if total - largest >= amount - 1 else 0
    given, surplus = [largest] + [least] * (amount - 1), total - largest - least * (amount - 1)
    while surplus > 0:
        movable = [i for i in range(1, amount) if given[i] < largest] or [i for i in range(1, amount) if given[i] < limit]
        mass, remaining = sum([portions[i] for i in movable]), surplus
        for i in movable:
            extra = min(limit - given[i], max(1, remaining * portions[i] // mass), surplus)
            given[i] = given[i] + extra
            surplus = surplus - extra
    return np.array(given)


def gaussian(own_key, extent, scale, limit, cuts=(), held_as=jnp.bfloat16):
    drawn = jax.random.normal(own_key, extent, jnp.float32) * scale
    if len(cuts) > 0:
        drawn = block_scale(own_key, extent, cuts, -0.22, 0.18) * drawn
    return jnp.clip(drawn, min=-limit, max=limit).astype(held_as)


def setup_inputs(seed: int = 0) -> dict:
    key_list = jax.random.split(jax.random.key(seed), 9)
    upstream = gaussian(key_list[0], (N_SECTION, TOKENS, D), 1.0, 6.0, ((0, 8), (1, 16)))
    routes_keys = jax.random.split(jax.random.fold_in(key_list[1], 1), N_SECTION * TOKENS // TOK_DEV)
    routes_turns = jax.random.permutation(jax.random.fold_in(key_list[1], 3), N_SECTION * TOKENS // TOK_DEV)
    routes = jax.vmap(lambda own, number: deal_out(jax.random.fold_in(key_list[1], 2), own, number, TOK_DEV, E_WIN, TOPK, CAP, 1))(routes_keys, routes_turns).reshape((N_SECTION, TOKENS, TOPK))
    combine_weights = jnp.clip(0.049804688 + 0.9501953 * jax.random.uniform(key_list[2], (N_SECTION, TOKENS, TOPK), jnp.float32) ** block_scale(key_list[2], (N_SECTION, TOKENS, TOPK), ((0, 8), (1, 16)), -0.2, 0.2), 0.049804688, 1.0).astype(jnp.bfloat16)
    gate_saved = gaussian(key_list[3], (N_SECTION, N_EP, CAP, E_WIN * FF), 0.5, 3.0, ((0, 8), (3, 16)))
    up_saved = gaussian(key_list[4], (N_SECTION, N_EP, CAP, E_WIN * FF), 0.5, 3.0, ((0, 8), (3, 16)))
    w_gate = gaussian(key_list[5], (N_SECTION, D, E_WIN * FF), D ** -0.5, 0.0625, ((0, 8), (2, 16)))
    w_up = gaussian(key_list[6], (N_SECTION, D, E_WIN * FF), D ** -0.5, 0.0625, ((0, 8), (2, 16)))
    w_down = gaussian(key_list[7], (N_SECTION, E_WIN * FF, D), FF ** -0.5, 0.1875, ((0, 8), (1, 16)))
    return dict(upstream=upstream, routes=routes, combine_weights=combine_weights, gate_saved=gate_saved, up_saved=up_saved, w_gate=w_gate, w_up=w_up, w_down=w_down)


def slot_tables(routes_local, weights_local, tok_count):
    flat_routes = routes_local.reshape(-1).astype(jnp.int32)
    flat_weights = weights_local.reshape(-1)
    entries = flat_routes.shape[0]
    onehot = (flat_routes[:, None] == jnp.arange(E_WIN, dtype=jnp.int32)[None, :]).astype(jnp.int32)
    slot_rank = jnp.sum((jnp.cumsum(onehot, axis=0) - onehot) * onehot, axis=1)
    positions = (flat_routes * CAP + slot_rank).astype(jnp.int32)
    token_of = jnp.arange(entries, dtype=jnp.int32) // TOPK
    slot_token = jnp.full((E_WIN * CAP,), tok_count, jnp.int32).at[positions].set(token_of)
    slot_weight = jnp.zeros((E_WIN * CAP,), weights_local.dtype).at[positions].set(flat_weights)
    return positions, slot_token, slot_weight


def take_rows(source, index):
    return jnp.take(source, index, axis=0, mode="fill", fill_value=0)


def add_rows(base, index, values):
    return base.at[index].add(values, mode="drop")


def slice_terms(expert_rows, weight, gate_part, up_part, gate_cols, up_cols, down_rows):
    gate_vals = gate_part.astype(jnp.float32)
    up_vals = up_part.astype(jnp.float32)
    back_grad = jnp.einsum("scd,hd->sch", expert_rows.astype(jnp.float32), down_rows.astype(jnp.float32))
    sigmoid_gate = jax.nn.sigmoid(gate_vals)
    silu_gate = gate_vals * sigmoid_gate
    hidden_act = silu_gate * up_vals
    router_part = jnp.sum(hidden_act * back_grad, axis=-1).astype(jnp.bfloat16)
    scaled = back_grad * weight.astype(jnp.float32)[:, :, None]
    grad_gate = (scaled * up_vals * sigmoid_gate * (1.0 + gate_vals * (1.0 - sigmoid_gate))).astype(jnp.bfloat16)
    grad_up = (scaled * silu_gate).astype(jnp.bfloat16)
    input_part = jnp.einsum("sch,dh->scd", grad_gate.astype(jnp.float32), gate_cols.astype(jnp.float32))
    input_part = input_part + jnp.einsum("sch,dh->scd", grad_up.astype(jnp.float32), up_cols.astype(jnp.float32))
    return input_part.astype(jnp.bfloat16), router_part


def reference(upstream, routes, combine_weights, gate_saved, up_saved, w_gate, w_up, w_down):
    slices = N_EP // E_WIN
    hid_dev = FF // slices
    grad_list = []
    router_list = []
    for section_idx in range(N_SECTION):
        grad_section = upstream[(section_idx + 1) % N_SECTION].reshape(N_EP, TOK_DEV, D)
        route_blocks = routes[section_idx].reshape(N_EP, TOK_DEV, TOPK)
        weight_blocks = combine_weights[section_idx].reshape(N_EP, TOK_DEV, TOPK)
        positions, slot_token, slot_weight = jax.vmap(partial(slot_tables, tok_count=TOK_DEV))(route_blocks, weight_blocks)
        packed = jax.vmap(take_rows)(grad_section, slot_token)
        input_sum = jnp.zeros((N_EP, E_WIN * CAP, D), jnp.float32)
        router_sum = jnp.zeros((N_EP, E_WIN * CAP), jnp.float32)
        for expert_idx in range(E_WIN):
            offset = expert_idx * CAP
            expert_rows = packed[:, offset:offset + CAP]
            weight = slot_weight[:, offset:offset + CAP]
            input_acc = jnp.zeros((N_EP, CAP, D), jnp.float32)
            router_acc = jnp.zeros((N_EP, CAP), jnp.float32)
            for slice_idx in range(slices):
                column = expert_idx * FF + slice_idx * hid_dev
                input_part, router_part = slice_terms(
                    expert_rows, weight,
                    gate_saved[section_idx, :, :, column:column + hid_dev],
                    up_saved[section_idx, :, :, column:column + hid_dev],
                    w_gate[section_idx, :, column:column + hid_dev],
                    w_up[section_idx, :, column:column + hid_dev],
                    w_down[section_idx, column:column + hid_dev])
                input_acc = input_acc + input_part.astype(jnp.float32)
                router_acc = router_acc + router_part.astype(jnp.float32)
            input_sum = input_sum.at[:, offset:offset + CAP].set(input_acc)
            router_sum = router_sum.at[:, offset:offset + CAP].set(router_acc)
        combined = jax.vmap(add_rows)(grad_section.astype(jnp.float32), slot_token, input_sum)
        grad_list.append(combined.astype(jnp.bfloat16).reshape(TOKENS, D))
        router_list.append(jnp.take_along_axis(router_sum, positions, axis=1).reshape(TOKENS, TOPK))
    return jnp.stack(grad_list), jnp.stack(router_list)
```

```python
import functools

import jax
import jax.numpy as jnp
from jax import lax
from jax.experimental import pallas as pl
from jax.experimental.pallas import tpu as pltpu
from jax.sharding import PartitionSpec as P

MESH = pl.DeviceIdType.MESH
BF = jnp.bfloat16
F32 = jnp.float32

SECTIONS = 8
E_WIN = 4
SLICES = 4
TOPK = 2
CAP = 80
TOK = 128
D = 7168
HID = 256
Q = D // SLICES
ROWS = SLICES * CAP

CW = 512
CA = 4096
NA = CA // CW
HA = NA // 2
NB = (D - CA) // CW
HB = NB // 2
RT = 128
WA = CA + RT
BCOL = WA
WB = D - CA


def dot_nt(a, b):
    return lax.dot_general(a, b, (((1,), (1,)), ((), ())), preferred_element_type=F32)


def place():
    s = lax.axis_index("section")
    p = lax.axis_index("ep")
    return s, p // SLICES, lax.rem(p, SLICES)


def shifted(a, by, n):
    return lax.rem(a + by + n, n)


def cols(start, width):
    return pl.ds(pl.multiple_of(start, 128), width)


def remote(src, dst, send, recv, device):
    return pltpu.make_async_remote_copy(
        src_ref=src, dst_ref=dst, send_sem=send, recv_sem=recv, device_id=device, device_id_type=MESH
    )


def dispatch_kernel(
    up, wd, pick, cot, bp,
    tok, slots, recv, wdr, ps,
    tok_s, tok_r, wd_s, wd_r, cot_s, cot_r, y_s, y_r, b_s, b_r, loc,
):
    s, y, z = place()
    behind = shifted(s, -1, SECTIONS)
    ahead = shifted(s, 1, SECTIONS)

    def dev(section, yy, zz):
        return (section, yy * SLICES + zz)

    barrier = pltpu.get_barrier_semaphore()
    for k in range(SLICES):
        pl.semaphore_signal(barrier, inc=1, device_id=dev(ahead, y, k), device_id_type=MESH)
    for k in range(1, SLICES):
        pl.semaphore_signal(barrier, inc=1, device_id=dev(s, y, shifted(z, k, SLICES)), device_id_type=MESH)
        pl.semaphore_signal(barrier, inc=1, device_id=dev(s, shifted(y, k, E_WIN), z), device_id_type=MESH)
    pl.semaphore_wait(barrier, 10)

    def tok_copy(k, owner):
        q = shifted(z, k, SLICES)
        return remote(up.at[:, cols(q * Q, Q)], tok.at[owner], tok_s.at[k], tok_r.at[k], dev(behind, y, q))

    def wd_copy(k, owner):
        q = shifted(z, k, SLICES)
        return remote(wd.at[:, cols(q * Q, Q)], wdr.at[owner], wd_s.at[k], wd_r.at[k], dev(s, y, q))

    cot_copy = remote(up, cot, cot_s, cot_r, dev(behind, y, z))
    wd_own = pltpu.make_async_copy(wd.at[:, cols(z * Q, Q)], wdr.at[z], loc.at[0])

    def y_copy(k, m, source, owner):
        return remote(
            slots.at[k, m], recv.at[owner, source], y_s.at[k, m], y_r.at[k, m], dev(s, shifted(y, k, E_WIN), z)
        )

    def b_copy(k, m, yb, owner):
        return remote(
            ps.at[k, yb], bp.at[owner, yb], b_s.at[k, m], b_r.at[k, m], dev(s, y, shifted(z, k, SLICES))
        )

    for k in (2, 1, 3, 0):
        tok_copy(k, z).start()
    wd_own.start()

    order = (0, 1, 3, 2)
    for m in order:
        source = shifted(z, -m, SLICES)
        tok_copy(m, source).wait_recv()

        def pack(k, _):
            e = shifted(y, k, E_WIN)
            rows = jnp.dot(pick[source, e], tok[source], preferred_element_type=F32).astype(BF)
            slots[k, m] = rows
            y_copy(k, m, source, y).start()
            return 0

        lax.fori_loop(1, E_WIN, pack, 0)
        recv[y, source] = jnp.dot(pick[source, y], tok[source], preferred_element_type=F32).astype(BF)
        if m == order[-1]:
            for k in (2, 1, 3):
                wd_copy(k, z).start()
            cot_copy.start()

    wd_own.wait()
    for k in (1, 3, 2):
        wd_copy(k, shifted(z, -k, SLICES)).wait_recv()

    own = []
    for m in (0, 1, 3, 2):
        yb = shifted(y, -m, E_WIN)
        if m:
            for j in order:
                y_copy(m, j, shifted(z, -j, SLICES), yb).wait_recv()

        def partial_grad(k, _):
            h = shifted(z, k, SLICES)
            part = dot_nt(recv[yb].reshape(ROWS, Q), wdr[h])
            ps[k, yb] = part.astype(BF).reshape(SLICES, CAP, HID)
            b_copy(k, m, yb, z).start()
            return 0

        lax.fori_loop(1, SLICES, partial_grad, 0)
        part = dot_nt(recv[yb].reshape(ROWS, Q), wdr[z])
        ps[0, yb] = part.astype(BF).reshape(SLICES, CAP, HID)
        copy = pltpu.make_async_copy(ps.at[0, yb], bp.at[z, yb], loc.at[1 + m])
        copy.start()
        own.append(copy)

    for copy in own:
        copy.wait()
    for k in range(SLICES):
        tok_copy(k, z).wait_send()
    cot_copy.wait()
    for k in range(1, SLICES):
        wd_copy(k, z).wait_send()
        for m in range(SLICES):
            y_copy(k, m, shifted(z, -m, SLICES), y).wait_send()
        for m in range(E_WIN):
            yb = shifted(y, -m, E_WIN)
            b_copy(k, m, yb, z).wait_send()
            b_copy(k, m, yb, shifted(z, -k, SLICES)).wait_recv()


def return_kernel(
    bp, gate, upv, sw, wg, wu, cot, spread, spread_k, out, router,
    grads, weights, partial, r1p, r1m, r2p, r2m, arecv, brecv, ctok, rb1p, rb1m, rb2p, rb2m,
    w_sem, r1_s, r1_r, r2p_s, r2p_r, r2m_s, r2m_r, ay_s, ay_r, by_s, by_r, b1_s, b1_r, b2p_s, b2p_r, b2m_s, b2m_r,
):
    s, y, z = place()
    zp, zm, z2 = shifted(z, 1, SLICES), shifted(z, -1, SLICES), shifted(z, 2, SLICES)
    right, left = (s, y * SLICES + zp), (s, y * SLICES + zm)

    def along_y(k):
        return (s, shifted(y, k, E_WIN) * SLICES + z)

    def w_copy(c):
        take = pl.ds(c * CW, CW)
        return (
            pltpu.make_async_copy(wg.at[take], weights.at[c, :, pl.ds(0, HID)], w_sem.at[0, c]),
            pltpu.make_async_copy(wu.at[take], weights.at[c, :, pl.ds(HID, HID)], w_sem.at[1, c]),
        )

    def start_weights(c, _):
        for copy in w_copy(c):
            copy.start()
        return 0

    lax.fori_loop(0, D // CW, start_weights, 0)

    barrier = pltpu.get_barrier_semaphore()
    for device in (right, left, along_y(1), along_y(2), along_y(3)):
        pl.semaphore_signal(barrier, inc=1, device_id=device, device_id_type=MESH)

    def elementwise(b, _):
        back = bp[0, b].astype(F32)
        for k in range(1, SLICES):
            back = back + bp[k, b].astype(F32)
        g = gate[b].astype(F32)
        u = upv[b].astype(F32)
        sig = 1.0 / (1.0 + jnp.exp(-g))
        silu = g * sig
        part = jnp.sum(silu * u * back, axis=-1, keepdims=True)
        lane = lax.broadcasted_iota(jnp.int32, (SLICES, CAP, RT), 2)
        partial[b, :, :, pl.ds(CA, RT)] = jnp.where(lane == z, part, 0.0).astype(BF)
        scaled = back * sw[b]
        grad_gate = (scaled * u * sig * (1.0 + g * (1.0 - sig))).astype(BF)
        grad_up = (scaled * silu).astype(BF)
        grads[b, :, pl.ds(0, HID)] = grad_gate.reshape(ROWS, HID)
        grads[b, :, pl.ds(HID, HID)] = grad_up.reshape(ROWS, HID)
        return 0

    lax.fori_loop(0, E_WIN, elementwise, 0)

    pl.semaphore_wait(barrier, 5)

    def first(half, col, width, i):
        src = partial.at[:, z2, :, cols(col, width)]
        if half == 0:
            return remote(src, r1p.at[:, :, cols(col, width)], r1_s.at[i], r1_r.at[i], right)
        return remote(src, r1m.at[:, :, cols(col - CA // 2, width)], r1_s.at[i], r1_r.at[i], left)

    def to_right(col, width, i):
        src = partial.at[:, zp, :, cols(col, width)]
        return remote(src, r2p.at[:, :, cols(col, width)], r2p_s.at[i], r2p_r.at[i], right)

    def to_left(col, width, i):
        src = partial.at[:, zm, :, cols(col, width)]
        return remote(src, r2m.at[:, :, cols(col, width)], r2m_s.at[i], r2m_r.at[i], left)

    def a_copy(k, col, width, i):
        src = partial.at[shifted(y, k, E_WIN), z, :, cols(col, width)]
        return remote(src, arecv.at[y, :, cols(col, width)], ay_s.at[k, i], ay_r.at[k, i], along_y(k))

    def b_copy(k, j):
        src = partial.at[shifted(y, k, E_WIN), :, :, cols(BCOL + j * CW, CW)]
        return remote(src, brecv.at[:, y, :, cols(j * CW, CW)], by_s.at[k, j], by_r.at[k, j], along_y(k))

    def b_first(half, j):
        src = ctok.at[z2, :, cols(j * CW, CW)]
        if half == 0:
            return remote(src, rb1p.at[:, cols(j * CW, CW)], b1_s.at[j], b1_r.at[j], right)
        return remote(src, rb1m.at[:, cols((j - HB) * CW, CW)], b1_s.at[j], b1_r.at[j], left)

    def b_right(j):
        return remote(ctok.at[zp, :, cols(j * CW, CW)], rb2p.at[:, cols(j * CW, CW)], b2p_s.at[j], b2p_r.at[j], right)

    def b_left(j):
        return remote(ctok.at[zm, :, cols(j * CW, CW)], rb2m.at[:, cols(j * CW, CW)], b2m_s.at[j], b2m_r.at[j], left)

    first(1, CA, RT, NA).start()
    to_right(CA, RT, NA).start()

    def input_part(c, col):
        for copy in w_copy(c):
            copy.wait()

        def block(b, _):
            part = dot_nt(grads[b], weights[c])
            partial[b, :, :, cols(col, CW)] = part.astype(BF).reshape(SLICES, CAP, CW)
            return 0

        lax.fori_loop(0, E_WIN, block, 0)

    def produce_a(c, half):
        input_part(c, c * CW)
        first(half, c * CW, CW, c).start()
        if half == 0:
            to_left(c * CW, CW, c).start()
        else:
            to_right(c * CW, CW, c).start()

    def produce_b(j):
        input_part(NA + j, BCOL + j * CW)
        for k in (2, 1, 3):
            b_copy(k, j).start()
        brecv[:, y, :, cols(j * CW, CW)] = partial[y, :, :, cols(BCOL + j * CW, CW)]

    def produce(i, _):
        produce_a(i, 0)
        produce_a(HA + i, 1)
        produce_b(i)
        return 0

    lax.fori_loop(0, HA, produce, 0)

    def produce_rest(j, _):
        produce_b(j)
        return 0

    lax.fori_loop(HA, NB, produce_rest, 0)

    def relay(half, col, width, i):
        first(half, col, width, i).wait_recv()
        if half == 0:
            mine, other = partial.at[:, zp, :, cols(col, width)], r1p.at[:, :, cols(col, width)]
        else:
            mine, other = partial.at[:, zm, :, cols(col, width)], r1m.at[:, :, cols(col - CA // 2, width)]
        mine[...] = (mine[...].astype(F32) + other[...].astype(F32)).astype(BF)
        if half == 0:
            to_right(col, width, i).start()
        else:
            to_left(col, width, i).start()

    relay(1, CA, RT, NA)

    def relay_pair(i, _):
        relay(0, i * CW, CW, i)
        relay(1, (HA + i) * CW, CW, HA + i)
        return 0

    lax.fori_loop(0, HA, relay_pair, 0)

    def finish_a(col, width, i):
        to_right(col, width, i).wait_recv()
        to_left(col, width, i).wait_recv()
        mine = partial.at[:, z, :, cols(col, width)]
        total = mine[...].astype(F32) + r2p[:, :, cols(col, width)].astype(F32) + r2m[:, :, cols(col, width)].astype(F32)
        mine[...] = total.astype(BF)
        for k in (2, 1, 3):
            a_copy(k, col, width, i).start()
        arecv[y, :, cols(col, width)] = partial[y, z, :, cols(col, width)]

    def tokens_b(half, j):
        for k in (1, 3, 2):
            b_copy(k, j).wait_recv()

        def combine(zz, _):
            rows = brecv[zz, :, :, cols(j * CW, CW)].reshape(E_WIN * CAP, CW)
            ctok[zz, :, cols(j * CW, CW)] = jnp.dot(spread[zz], rows, preferred_element_type=F32).astype(BF)
            return 0

        lax.fori_loop(0, SLICES, combine, 0)
        b_first(half, j).start()
        if half == 0:
            b_left(j).start()
        else:
            b_right(j).start()

    finish_a(CA, RT, NA)

    def second(i, _):
        tokens_b(0, i)
        finish_a(i * CW, CW, i)
        tokens_b(1, HB + i)
        finish_a((HA + i) * CW, CW, HA + i)
        return 0

    lax.fori_loop(0, HB, second, 0)
    for i in range(HB, HA):
        finish_a(i * CW, CW, i)
        finish_a((HA + i) * CW, CW, HA + i)

    def relay_b(half, j):
        b_first(half, j).wait_recv()
        if half == 0:
            mine, other = ctok.at[zp, :, cols(j * CW, CW)], rb1p.at[:, cols(j * CW, CW)]
        else:
            mine, other = ctok.at[zm, :, cols(j * CW, CW)], rb1m.at[:, cols((j - HB) * CW, CW)]
        mine[...] = (mine[...].astype(F32) + other[...].astype(F32)).astype(BF)
        if half == 0:
            b_right(j).start()
        else:
            b_left(j).start()

    def relay_b_pair(i, _):
        relay_b(0, i)
        relay_b(1, HB + i)
        return 0

    lax.fori_loop(0, HB, relay_b_pair, 0)

    for k in range(1, E_WIN):
        a_copy(k, CA, RT, NA).wait_recv()
    parts = arecv[:, :, pl.ds(CA, RT)].reshape(E_WIN * CAP, RT)
    for k in range(TOPK):
        values = jnp.dot(spread_k[k], parts, preferred_element_type=F32)
        router[:, pl.ds(k, 1)] = jnp.sum(values, axis=-1, keepdims=True)

    def last_a(c, _):
        for k in (1, 3, 2):
            a_copy(k, c * CW, CW, c).wait_recv()
        rows = arecv[:, :, cols(c * CW, CW)].reshape(E_WIN * CAP, CW)
        total = jnp.dot(spread[z], rows, preferred_element_type=F32)
        out[:, cols(c * CW, CW)] = (cot[:, cols(c * CW, CW)].astype(F32) + total).astype(BF)
        return 0

    lax.fori_loop(0, NA, last_a, 0)

    def last_b(j, _):
        b_right(j).wait_recv()
        b_left(j).wait_recv()
        take = cols(j * CW, CW)
        total = ctok[z, :, take].astype(F32) + rb2p[:, take].astype(F32) + rb2m[:, take].astype(F32)
        out[:, cols(CA + j * CW, CW)] = (cot[:, cols(CA + j * CW, CW)].astype(F32) + total).astype(BF)
        return 0

    lax.fori_loop(0, NB, last_b, 0)

    def sent_a(half, col, width, i):
        first(half, col, width, i).wait_send()
        to_right(col, width, i).wait_send()
        to_left(col, width, i).wait_send()
        for k in range(1, E_WIN):
            a_copy(k, col, width, i).wait_send()

    def sent_a_pair(i, _):
        sent_a(0, i * CW, CW, i)
        sent_a(1, (HA + i) * CW, CW, HA + i)
        return 0

    lax.fori_loop(0, HA, sent_a_pair, 0)
    sent_a(1, CA, RT, NA)

    def sent_b(half, j):
        for k in range(1, E_WIN):
            b_copy(k, j).wait_send()
        b_first(half, j).wait_send()
        b_right(j).wait_send()
        b_left(j).wait_send()

    def sent_b_pair(i, _):
        sent_b(0, i)
        sent_b(1, HB + i)
        return 0

    lax.fori_loop(0, HB, sent_b_pair, 0)


def vmem(*shape, dtype=BF):
    return pltpu.VMEM(shape, dtype)


def sems(*shape):
    return pltpu.SemaphoreType.DMA(shape)


ANY = pl.BlockSpec(memory_space=pl.ANY)
VM = pl.BlockSpec(memory_space=pltpu.VMEM)


def dispatch(upstream, w_down, pick):
    return pl.pallas_call(
        dispatch_kernel,
        out_shape=(
            jax.ShapeDtypeStruct((TOK, D), BF),
            jax.ShapeDtypeStruct((SLICES, E_WIN, SLICES, CAP, HID), BF),
        ),
        in_specs=[ANY, ANY, VM],
        out_specs=(ANY, ANY),
        scratch_shapes=[
            vmem(SLICES, TOK, Q),
            vmem(E_WIN, SLICES, CAP, Q),
            vmem(E_WIN, SLICES, CAP, Q),
            vmem(SLICES, HID, Q),
            vmem(SLICES, E_WIN, SLICES, CAP, HID),
            sems(SLICES), sems(SLICES),
            sems(SLICES), sems(SLICES),
            pltpu.SemaphoreType.DMA, pltpu.SemaphoreType.DMA,
            sems(E_WIN, SLICES), sems(E_WIN, SLICES),
            sems(SLICES, E_WIN), sems(SLICES, E_WIN),
            sems(1 + E_WIN),
        ],
        compiler_params=pltpu.CompilerParams(collective_id=0, has_side_effects=True, vmem_limit_bytes=40 * 2**20),
        name="dispatch",
    )(upstream, w_down, pick)


def give_back(bp, gate, up, sw, w_gate, w_up, cot, spread, spread_k):
    return pl.pallas_call(
        return_kernel,
        out_shape=(
            jax.ShapeDtypeStruct((TOK, D), BF),
            jax.ShapeDtypeStruct((TOK, TOPK), F32),
        ),
        in_specs=[VM, VM, VM, VM, ANY, ANY, VM, VM, VM],
        out_specs=(VM, VM),
        scratch_shapes=[
            vmem(E_WIN, ROWS, 2 * HID),
            vmem(D // CW, CW, 2 * HID),
            vmem(E_WIN, SLICES, CAP, D + RT),
            vmem(E_WIN, CAP, CA // 2),
            vmem(E_WIN, CAP, CA // 2 + RT),
            vmem(E_WIN, CAP, WA),
            vmem(E_WIN, CAP, WA),
            vmem(E_WIN, CAP, WA),
            vmem(SLICES, E_WIN, CAP, WB),
            vmem(SLICES, TOK, WB),
            vmem(TOK, WB // 2),
            vmem(TOK, WB // 2),
            vmem(TOK, WB),
            vmem(TOK, WB),
            sems(2, D // CW),
            sems(NA + 1), sems(NA + 1),
            sems(NA + 1), sems(NA + 1),
            sems(NA + 1), sems(NA + 1),
            sems(E_WIN, NA + 1), sems(E_WIN, NA + 1),
            sems(E_WIN, NB), sems(E_WIN, NB),
            sems(NB), sems(NB),
            sems(NB), sems(NB),
            sems(NB), sems(NB),
        ],
        compiler_params=pltpu.CompilerParams(collective_id=1, has_side_effects=True, vmem_limit_bytes=63 * 2**20),
        name="give_back",
    )(bp, gate, up, sw, w_gate, w_up, cot, spread, spread_k)


def local(upstream, routes, combine_weights, gate_saved, up_saved, w_gate, w_up, w_down):
    p = lax.axis_index("ep")
    y, z = p // SLICES, lax.rem(p, SLICES)
    info = jnp.concatenate([routes[0].astype(F32).T, combine_weights[0].astype(F32).T], axis=0)
    gathered = lax.all_gather(info, "ep")
    named = gathered[:, :TOPK]
    gains = gathered[:, TOPK:]
    experts = jnp.arange(E_WIN, dtype=F32)
    hit = (named[:, :, None, :] == experts[None, None, :, None]).sum(axis=1)
    before = jnp.triu(jnp.ones((TOK, TOK), BF), 1)
    rank = jnp.einsum("set,tu->seu", hit.astype(BF), before, preferred_element_type=F32)
    slot = jnp.where(hit > 0, rank, -1.0)
    slots = jnp.arange(CAP, dtype=F32)
    mine = lax.dynamic_index_in_dim(slot, y, 1, keepdims=False)
    gain = jnp.sum(jnp.where(named == y.astype(F32), gains, 0.0), axis=1)
    slot_weight = jnp.sum(jnp.where(mine[:, None, :] == slots[None, :, None], gain[:, None, :], 0.0), axis=-1)
    row = lax.dynamic_slice_in_dim(slot, y * SLICES, SLICES, 0)
    pick = (row[:, :, None, :] == slots[None, None, :, None]).astype(BF)
    spread = (jnp.swapaxes(row, 1, 2)[:, :, :, None] == slots[None, None, None, :]).astype(BF)
    own = lax.dynamic_index_in_dim(spread, z, 0, keepdims=False)
    chosen = routes[0].T[:, :, None, None] == jnp.arange(E_WIN, dtype=jnp.int32)[None, None, :, None]
    spread_k = jnp.where(chosen, own[None], 0).astype(BF).reshape(TOPK, TOK, E_WIN * CAP)

    cot, bp = dispatch(upstream[0], w_down[0], pick)
    grad_input, router_grad = give_back(
        bp,
        gate_saved[0].reshape(E_WIN, SLICES, CAP, HID),
        up_saved[0].reshape(E_WIN, SLICES, CAP, HID),
        slot_weight.reshape(E_WIN, SLICES, CAP, 1),
        w_gate[0],
        w_up[0],
        cot,
        spread.reshape(SLICES, TOK, E_WIN * CAP),
        spread_k,
    )
    return grad_input[None], router_grad[None]


def solution(mesh):
    in_specs = (
        P("section", "ep", None),
        P("section", "ep", None),
        P("section", "ep", None),
        P("section", None, None, "ep"),
        P("section", None, None, "ep"),
        P("section", None, "ep"),
        P("section", None, "ep"),
        P("section", "ep", None),
    )
    out_specs = (P("section", "ep", None), P("section", "ep", None))
    return jax.shard_map(local, mesh=mesh, in_specs=in_specs, out_specs=out_specs, check_vma=False)
```

```python
import jax
import jax.numpy as jnp
from jax import lax
from jax.experimental import pallas as pl
from jax.experimental.pallas import tpu as pltpu
from jax.sharding import PartitionSpec as P

MESH = pl.DeviceIdType.MESH
BF = jnp.bfloat16
F32 = jnp.float32

SECTIONS = 8
E_WIN = 4
SLICES = 4
TOPK = 2
CAP = 80
TOK = 128
D = 7168
HID = 256
Q = D // SLICES
ROWS = SLICES * CAP
NQ = 2
QH = Q // NQ

CW = 512
CA = 4096
NA = CA // CW
HA = NA // 2
NB = (D - CA) // CW
HB = NB // 2
RT = 128
WA = CA + RT
BCOL = WA
WB = D - CA


def dot_nt(a, b):
    return lax.dot_general(a, b, (((1,), (1,)), ((), ())), preferred_element_type=F32)


def place():
    s = lax.axis_index("section")
    p = lax.axis_index("ep")
    return s, p // SLICES, lax.rem(p, SLICES)


def shifted(a, by, n):
    return lax.rem(a + by + n, n)


def cols(start, width):
    return pl.ds(pl.multiple_of(start, 128), width)


def remote(src, dst, send, recv, device):
    return pltpu.make_async_remote_copy(
        src_ref=src, dst_ref=dst, send_sem=send, recv_sem=recv, device_id=device, device_id_type=MESH
    )


def layer_kernel(
    up, routes, gains, gate, upv, wg, wu, wd, out, router,
    info, slot_gain, pick, spread, gate_v, up_v, wdr, cot,
    grads, weights, partial, r1p, r1m, r2p, r2m, arecv, brecv, ctok, rb1p, rb1m, rb2p, rb2m,
    iz_s, iz_r, iy_s, iy_r, tok_s, tok_r, wd_s, wd_r, cot_s, cot_r, y_s, y_r, g_s, g_r, loc, out_s,
    w_sem, r1_s, r1_r, r2p_s, r2p_r, r2m_s, r2m_r, ay_s, ay_r, by_s, by_r, b1_s, b1_r, b2p_s, b2p_r, b2m_s, b2m_r,
):
    s, y, z = place()
    behind = shifted(s, -1, SECTIONS)
    ahead = shifted(s, 1, SECTIONS)
    zp, zm, z2 = shifted(z, 1, SLICES), shifted(z, -1, SLICES), shifted(z, 2, SLICES)

    def along_z(k):
        return (s, y * SLICES + shifted(z, k, SLICES))

    def along_y(k):
        return (s, shifted(y, k, E_WIN) * SLICES + z)

    right, left = along_z(1), along_z(3)

    barrier = pltpu.get_barrier_semaphore()
    for k in range(SLICES):
        pl.semaphore_signal(barrier, inc=1, device_id=(ahead, y * SLICES + k), device_id_type=MESH)
    for k in range(1, SLICES):
        pl.semaphore_signal(barrier, inc=1, device_id=along_z(k), device_id_type=MESH)
        pl.semaphore_signal(barrier, inc=1, device_id=along_y(k), device_id_type=MESH)

    def w_copy(c):
        take = pl.ds(c * CW, CW)
        return (
            pltpu.make_async_copy(wg.at[take], weights.at[c, :, pl.ds(0, HID)], w_sem.at[0, c]),
            pltpu.make_async_copy(wu.at[take], weights.at[c, :, pl.ds(HID, HID)], w_sem.at[1, c]),
        )

    wd_own = pltpu.make_async_copy(wd.at[:, cols(z * Q, Q)], wdr.at[z], loc.at[0])
    saved = (pltpu.make_async_copy(gate, gate_v, loc.at[1]), pltpu.make_async_copy(upv, up_v, loc.at[2]))

    info[y, z] = jnp.concatenate(
        [routes[...].astype(F32), gains[...].astype(F32), jnp.zeros((8 - 2 * TOPK, TOK), F32)], axis=0
    )
    row8 = lax.broadcasted_iota(jnp.int32, (8, TOK), 0).astype(F32)
    later = lax.broadcasted_iota(jnp.int32, (TOK, TOK), 1)
    earlier = lax.broadcasted_iota(jnp.int32, (TOK, TOK), 0)
    before = (earlier < later).astype(F32).astype(BF)
    unit = (earlier == later).astype(F32).astype(BF)
    slot_row = lax.broadcasted_iota(jnp.int32, (CAP, TOK), 0).astype(F32)

    pl.semaphore_wait(barrier, 10)

    def slots(k, m):
        return partial.at[k, m, :, pl.ds(0, Q)]

    def recv(owner, source):
        return partial.at[owner, source, :, pl.ds(Q, Q)]

    def ps(k, yb):
        return partial.at[yb, :, :, cols(2 * Q + (SLICES + k) * HID, HID)]

    def bp(owner, yb):
        return partial.at[yb, :, :, cols(2 * Q + owner * HID, HID)]

    def tok(source, h):
        return ctok.at[source, :, pl.ds(h * QH, QH)]

    def info_z(k, owner):
        return remote(info.at[y, z], info.at[y, owner], iz_s.at[k], iz_r.at[k], along_z(k))

    def info_y(k, owner):
        return remote(info.at[y], info.at[owner], iy_s.at[k], iy_r.at[k], along_y(k))

    def tok_copy(k, h, owner):
        q = shifted(z, k, SLICES)
        return remote(
            up.at[:, cols(q * Q + h * QH, QH)], tok(owner, h), tok_s.at[k, h], tok_r.at[k, h], (behind, y * SLICES + q)
        )

    def wd_copy(k, owner):
        q = shifted(z, k, SLICES)
        return remote(wd.at[:, cols(q * Q, Q)], wdr.at[owner], wd_s.at[k], wd_r.at[k], along_z(k))

    cot_copy = remote(up, cot, cot_s, cot_r, (behind, y * SLICES + z))

    def y_copy(k, m, h, source, owner):
        return remote(
            slots(k, m).at[:, pl.ds(h * QH, QH)],
            recv(owner, source).at[:, pl.ds(h * QH, QH)],
            y_s.at[k, m, h], y_r.at[k, m, h], along_y(k),
        )

    def g_copy(k, m, yb, owner):
        return remote(ps(k, yb), bp(owner, yb), g_s.at[k, m], g_r.at[k, m], along_z(k))

    for k in (2, 1, 3):
        info_z(k, z).start()
    for h in range(NQ):
        for k in (2, 1, 3, 0):
            tok_copy(k, h, z).start()
    wd_own.start()
    for copy in saved:
        copy.start()

    def start_weights(c, _):
        for copy in w_copy(c):
            copy.start()
        return 0

    lax.fori_loop(0, D // CW, start_weights, 0)

    for k in (1, 3, 2):
        info_z(k, shifted(z, -k, SLICES)).wait_recv()
    for k in (2, 1, 3):
        info_y(k, y).start()

    def slot_of(block):
        hit = (block[0:1] == row8) | (block[1:2] == row8)
        rank = jnp.dot(hit.astype(F32).astype(BF), before, preferred_element_type=F32)
        return jnp.where(hit, rank, -1.0)

    def row_tables(zz, _):
        slot = slot_of(info[y, zz])
        for e in range(E_WIN):
            pick[zz, e] = (slot_row == slot[e:e + 1]).astype(F32).astype(BF)
        spread[zz] = dot_nt(unit, pick[zz].reshape(E_WIN * CAP, TOK)).astype(BF)
        return 0

    lax.fori_loop(0, SLICES, row_tables, 0)

    order = (0, 1, 3, 2)
    for h in range(NQ):
        for m in order:
            source = shifted(z, -m, SLICES)
            tok_copy(m, h, source).wait_recv()
            if h == NQ - 1 and m == order[-1]:
                for k in (2, 1, 3):
                    wd_copy(k, z).start()
                cot_copy.start()

            def pack(k, _):
                e = shifted(y, k, E_WIN)
                rows = jnp.dot(pick[source, e], tok(source, h)[...], preferred_element_type=F32).astype(BF)
                slots(k, m).at[:, pl.ds(h * QH, QH)][...] = rows
                y_copy(k, m, h, source, y).start()
                return 0

            lax.fori_loop(1, E_WIN, pack, 0)
            rows = jnp.dot(pick[source, y], tok(source, h)[...], preferred_element_type=F32).astype(BF)
            recv(y, source).at[:, pl.ds(h * QH, QH)][...] = rows

    for k in (1, 3, 2):
        info_y(k, shifted(y, -k, E_WIN)).wait_recv()

    def expert_tables(i, _):
        b, zz = i // SLICES, lax.rem(i, SLICES)
        block = info[b, zz]
        here = y.astype(F32)
        slot = jnp.sum(jnp.where(row8 == here, slot_of(block), 0.0), axis=0, keepdims=True)
        gain = jnp.where(block[0:1] == here, block[2:3], 0.0) + jnp.where(block[1:2] == here, block[3:4], 0.0)
        slot_gain[b, zz, pl.ds(0, 1)] = slot
        slot_gain[b, zz, pl.ds(1, 1)] = gain
        return 0

    lax.fori_loop(0, E_WIN * SLICES, expert_tables, 0)

    wd_own.wait()
    for k in (1, 3, 2):
        wd_copy(k, shifted(z, -k, SLICES)).wait_recv()

    own = []
    for m in (0, 1, 3, 2):
        yb = shifted(y, -m, E_WIN)
        if m:
            for h in range(NQ):
                for j in order:
                    y_copy(m, j, h, shifted(z, -j, SLICES), yb).wait_recv()

        def rows_of():
            return partial[yb, :, :, pl.ds(Q, Q)].reshape(ROWS, Q)

        def partial_grad(k, _):
            part = dot_nt(rows_of(), wdr[shifted(z, k, SLICES)])
            ps(k, yb)[...] = part.astype(BF).reshape(SLICES, CAP, HID)
            g_copy(k, m, yb, z).start()
            return 0

        lax.fori_loop(1, SLICES, partial_grad, 0)
        bp(z, yb)[...] = dot_nt(rows_of(), wdr[z]).astype(BF).reshape(SLICES, CAP, HID)

    for copy in saved:
        copy.wait()

    for m in (0, 1, 3, 2):
        yb = shifted(y, -m, E_WIN)
        for k in (1, 3, 2):
            g_copy(k, m, yb, shifted(z, -k, SLICES)).wait_recv()

        def elementwise(zz, _):
            back = partial[yb, zz, :, pl.ds(2 * Q, HID)].astype(F32)
            for k in range(1, SLICES):
                back = back + partial[yb, zz, :, pl.ds(2 * Q + k * HID, HID)].astype(F32)
            g = gate_v[yb * SLICES + zz].astype(F32)
            u = up_v[yb * SLICES + zz].astype(F32)
            held = slot_row == slot_gain[yb, zz, pl.ds(0, 1)]
            gain = jnp.sum(jnp.where(held, slot_gain[yb, zz, pl.ds(1, 1)], 0.0), axis=-1, keepdims=True)
            sig = 1.0 / (1.0 + jnp.exp(-g))
            silu = g * sig
            part = jnp.sum(silu * u * back, axis=-1, keepdims=True)
            lane = lax.broadcasted_iota(jnp.int32, (CAP, RT), 1)
            partial[yb, zz, :, pl.ds(CA, RT)] = jnp.where(lane == z, part, 0.0).astype(BF)
            scaled = back * gain
            grads[yb, zz, :, pl.ds(0, HID)] = (scaled * u * sig * (1.0 + g * (1.0 - sig))).astype(BF)
            grads[yb, zz, :, pl.ds(HID, HID)] = (scaled * silu).astype(BF)
            return 0

        lax.fori_loop(0, SLICES, elementwise, 0)

    for k in range(1, SLICES):
        for m in range(SLICES):
            for h in range(NQ):
                y_copy(k, m, h, shifted(z, -m, SLICES), y).wait_send()
            g_copy(k, m, shifted(y, -m, E_WIN), z).wait_send()

    def first(half, col, width, i):
        src = partial.at[:, z2, :, cols(col, width)]
        if half == 0:
            return remote(src, r1p.at[:, :, cols(col, width)], r1_s.at[i], r1_r.at[i], right)
        return remote(src, r1m.at[:, :, cols(col - CA // 2, width)], r1_s.at[i], r1_r.at[i], left)

    def to_right(col, width, i):
        src = partial.at[:, zp, :, cols(col, width)]
        return remote(src, r2p.at[:, :, cols(col, width)], r2p_s.at[i], r2p_r.at[i], right)

    def to_left(col, width, i):
        src = partial.at[:, zm, :, cols(col, width)]
        return remote(src, r2m.at[:, :, cols(col, width)], r2m_s.at[i], r2m_r.at[i], left)

    def a_copy(k, col, width, i):
        src = partial.at[shifted(y, k, E_WIN), z, :, cols(col, width)]
        return remote(src, arecv.at[y, :, cols(col, width)], ay_s.at[k, i], ay_r.at[k, i], along_y(k))

    def b_copy(k, j):
        src = partial.at[shifted(y, k, E_WIN), :, :, cols(BCOL + j * CW, CW)]
        return remote(src, brecv.at[:, y, :, cols(j * CW, CW)], by_s.at[k, j], by_r.at[k, j], along_y(k))

    def b_first(half, j):
        src = ctok.at[z2, :, cols(j * CW, CW)]
        if half == 0:
            return remote(src, rb1p.at[:, cols(j * CW, CW)], b1_s.at[j], b1_r.at[j], right)
        return remote(src, rb1m.at[:, cols((j - HB) * CW, CW)], b1_s.at[j], b1_r.at[j], left)

    def b_right(j):
        return remote(ctok.at[zp, :, cols(j * CW, CW)], rb2p.at[:, cols(j * CW, CW)], b2p_s.at[j], b2p_r.at[j], right)

    def b_left(j):
        return remote(ctok.at[zm, :, cols(j * CW, CW)], rb2m.at[:, cols(j * CW, CW)], b2m_s.at[j], b2m_r.at[j], left)

    first(1, CA, RT, NA).start()
    to_right(CA, RT, NA).start()

    def input_part(c, col):
        for copy in w_copy(c):
            copy.wait()

        def block(b, _):
            part = dot_nt(grads[b].reshape(ROWS, 2 * HID), weights[c])
            partial[b, :, :, cols(col, CW)] = part.astype(BF).reshape(SLICES, CAP, CW)
            return 0

        lax.fori_loop(0, E_WIN, block, 0)

    def produce_a(c, half):
        input_part(c, c * CW)
        first(half, c * CW, CW, c).start()
        if half == 0:
            to_left(c * CW, CW, c).start()
        else:
            to_right(c * CW, CW, c).start()

    def produce_b(j):
        input_part(NA + j, BCOL + j * CW)
        for k in (2, 1, 3):
            b_copy(k, j).start()
        brecv[:, y, :, cols(j * CW, CW)] = partial[y, :, :, cols(BCOL + j * CW, CW)]

    def produce(i, _):
        produce_a(i, 0)
        produce_a(HA + i, 1)
        produce_b(i)
        return 0

    lax.fori_loop(0, HA, produce, 0)

    def produce_rest(j, _):
        produce_b(j)
        return 0

    lax.fori_loop(HA, NB, produce_rest, 0)

    def relay(half, col, width, i):
        first(half, col, width, i).wait_recv()
        if half == 0:
            mine, other = partial.at[:, zp, :, cols(col, width)], r1p.at[:, :, cols(col, width)]
        else:
            mine, other = partial.at[:, zm, :, cols(col, width)], r1m.at[:, :, cols(col - CA // 2, width)]
        mine[...] = (mine[...].astype(F32) + other[...].astype(F32)).astype(BF)
        if half == 0:
            to_right(col, width, i).start()
        else:
            to_left(col, width, i).start()

    relay(1, CA, RT, NA)

    def relay_pair(i, _):
        relay(0, i * CW, CW, i)
        relay(1, (HA + i) * CW, CW, HA + i)
        return 0

    lax.fori_loop(0, HA, relay_pair, 0)

    def finish_a(col, width, i):
        to_right(col, width, i).wait_recv()
        to_left(col, width, i).wait_recv()
        mine = partial.at[:, z, :, cols(col, width)]
        total = mine[...].astype(F32) + r2p[:, :, cols(col, width)].astype(F32) + r2m[:, :, cols(col, width)].astype(F32)
        mine[...] = total.astype(BF)
        for k in (2, 1, 3):
            a_copy(k, col, width, i).start()
        arecv[y, :, cols(col, width)] = partial[y, z, :, cols(col, width)]

    def tokens_b(half, j):
        for k in (1, 3, 2):
            b_copy(k, j).wait_recv()

        def combine(zz, _):
            rows = brecv[zz, :, :, cols(j * CW, CW)].reshape(E_WIN * CAP, CW)
            ctok[zz, :, cols(j * CW, CW)] = jnp.dot(spread[zz], rows, preferred_element_type=F32).astype(BF)
            return 0

        lax.fori_loop(0, SLICES, combine, 0)
        b_first(half, j).start()
        if half == 0:
            b_left(j).start()
        else:
            b_right(j).start()

    finish_a(CA, RT, NA)

    def second(i, _):
        tokens_b(0, i)
        finish_a(i * CW, CW, i)
        tokens_b(1, HB + i)
        finish_a((HA + i) * CW, CW, HA + i)
        return 0

    lax.fori_loop(0, HB, second, 0)
    for i in range(HB, HA):
        finish_a(i * CW, CW, i)
        finish_a((HA + i) * CW, CW, HA + i)

    def relay_b(half, j):
        b_first(half, j).wait_recv()
        if half == 0:
            mine, other = ctok.at[zp, :, cols(j * CW, CW)], rb1p.at[:, cols(j * CW, CW)]
        else:
            mine, other = ctok.at[zm, :, cols(j * CW, CW)], rb1m.at[:, cols((j - HB) * CW, CW)]
        mine[...] = (mine[...].astype(F32) + other[...].astype(F32)).astype(BF)
        if half == 0:
            b_right(j).start()
        else:
            b_left(j).start()

    def relay_b_pair(i, _):
        relay_b(0, i)
        relay_b(1, HB + i)
        return 0

    lax.fori_loop(0, HB, relay_b_pair, 0)

    for k in range(1, E_WIN):
        a_copy(k, CA, RT, NA).wait_recv()
    parts = dot_nt(unit, arecv[:, :, pl.ds(CA, RT)].reshape(E_WIN * CAP, RT)).astype(BF)
    expert = lax.broadcasted_iota(jnp.int32, (E_WIN, CAP, TOK), 0)
    for k in range(TOPK):
        chosen = jnp.where(expert == routes[pl.ds(k, 1)].reshape(1, 1, TOK), pick[z].astype(F32), 0.0).astype(BF)
        values = jnp.dot(parts, chosen.reshape(E_WIN * CAP, TOK), preferred_element_type=F32)
        router[pl.ds(k, 1)] = jnp.sum(values, axis=0, keepdims=True)

    def out_copy(c):
        return pltpu.make_async_copy(cot.at[:, cols(c * CW, CW)], out.at[:, cols(c * CW, CW)], out_s.at[c])

    cot_copy.wait_recv()

    def last_a(c, _):
        for k in (1, 3, 2):
            a_copy(k, c * CW, CW, c).wait_recv()
        rows = arecv[:, :, cols(c * CW, CW)].reshape(E_WIN * CAP, CW)
        total = jnp.dot(spread[z], rows, preferred_element_type=F32)
        cot[:, cols(c * CW, CW)] = (cot[:, cols(c * CW, CW)].astype(F32) + total).astype(BF)
        out_copy(c).start()
        return 0

    lax.fori_loop(0, NA, last_a, 0)

    def last_b(j, _):
        b_right(j).wait_recv()
        b_left(j).wait_recv()
        take = cols(j * CW, CW)
        total = ctok[z, :, take].astype(F32) + rb2p[:, take].astype(F32) + rb2m[:, take].astype(F32)
        cot[:, cols(CA + j * CW, CW)] = (cot[:, cols(CA + j * CW, CW)].astype(F32) + total).astype(BF)
        out_copy(NA + j).start()
        return 0

    lax.fori_loop(0, NB, last_b, 0)

    def sent_a(half, col, width, i):
        first(half, col, width, i).wait_send()
        to_right(col, width, i).wait_send()
        to_left(col, width, i).wait_send()
        for k in range(1, E_WIN):
            a_copy(k, col, width, i).wait_send()

    def sent_a_pair(i, _):
        sent_a(0, i * CW, CW, i)
        sent_a(1, (HA + i) * CW, CW, HA + i)
        return 0

    lax.fori_loop(0, HA, sent_a_pair, 0)
    sent_a(1, CA, RT, NA)

    def sent_b(half, j):
        for k in range(1, E_WIN):
            b_copy(k, j).wait_send()
        b_first(half, j).wait_send()
        b_right(j).wait_send()
        b_left(j).wait_send()

    def sent_b_pair(i, _):
        sent_b(0, i)
        sent_b(1, HB + i)
        return 0

    lax.fori_loop(0, HB, sent_b_pair, 0)

    def written(c, _):
        out_copy(c).wait()
        return 0

    lax.fori_loop(0, D // CW, written, 0)

    cot_copy.wait_send()
    for k in range(1, SLICES):
        info_z(k, z).wait_send()
        info_y(k, y).wait_send()
        wd_copy(k, z).wait_send()
    for h in range(NQ):
        for k in range(SLICES):
            tok_copy(k, h, z).wait_send()


def vmem(*shape, dtype=BF):
    return pltpu.VMEM(shape, dtype)


def sems(*shape):
    return pltpu.SemaphoreType.DMA(shape)


ANY = pl.BlockSpec(memory_space=pl.ANY)
VM = pl.BlockSpec(memory_space=pltpu.VMEM)


def layer(upstream, routes, gains, gate, up, w_gate, w_up, w_down):
    return pl.pallas_call(
        layer_kernel,
        out_shape=(
            jax.ShapeDtypeStruct((TOK, D), BF),
            jax.ShapeDtypeStruct((TOPK, TOK), F32),
        ),
        in_specs=[ANY, VM, VM, ANY, ANY, ANY, ANY, ANY],
        out_specs=(ANY, VM),
        scratch_shapes=[
            vmem(E_WIN, SLICES, 8, TOK, dtype=F32),
            vmem(E_WIN, SLICES, 8, TOK, dtype=F32),
            vmem(SLICES, E_WIN, CAP, TOK),
            vmem(SLICES, TOK, E_WIN * CAP),
            vmem(E_WIN * SLICES, CAP, HID),
            vmem(E_WIN * SLICES, CAP, HID),
            vmem(SLICES, HID, Q),
            vmem(TOK, D),
            vmem(E_WIN, SLICES, CAP, 2 * HID),
            vmem(D // CW, CW, 2 * HID),
            vmem(E_WIN, SLICES, CAP, D + RT),
            vmem(E_WIN, CAP, CA // 2),
            vmem(E_WIN, CAP, CA // 2 + RT),
            vmem(E_WIN, CAP, WA),
            vmem(E_WIN, CAP, WA),
            vmem(E_WIN, CAP, WA),
            vmem(SLICES, E_WIN, CAP, WB),
            vmem(SLICES, TOK, WB),
            vmem(TOK, WB // 2),
            vmem(TOK, WB // 2),
            vmem(TOK, WB),
            vmem(TOK, WB),
            sems(SLICES), sems(SLICES),
            sems(E_WIN), sems(E_WIN),
            sems(SLICES, NQ), sems(SLICES, NQ),
            sems(SLICES), sems(SLICES),
            pltpu.SemaphoreType.DMA, pltpu.SemaphoreType.DMA,
            sems(E_WIN, SLICES, NQ), sems(E_WIN, SLICES, NQ),
            sems(SLICES, E_WIN), sems(SLICES, E_WIN),
            sems(3),
            sems(D // CW),
            sems(2, D // CW),
            sems(NA + 1), sems(NA + 1),
            sems(NA + 1), sems(NA + 1),
            sems(NA + 1), sems(NA + 1),
            sems(E_WIN, NA + 1), sems(E_WIN, NA + 1),
            sems(E_WIN, NB), sems(E_WIN, NB),
            sems(NB), sems(NB),
            sems(NB), sems(NB),
            sems(NB), sems(NB),
        ],
        compiler_params=pltpu.CompilerParams(collective_id=0, has_side_effects=True, vmem_limit_bytes=63 * 2**20),
        name="layer",
    )(upstream, routes, gains, gate, up, w_gate, w_up, w_down)


def local(upstream, routes, combine_weights, gate_saved, up_saved, w_gate, w_up, w_down):
    grad_input, router_grad = layer(
        upstream[0], routes[0].T, combine_weights[0].T, gate_saved[0], up_saved[0], w_gate[0], w_up[0], w_down[0]
    )
    return grad_input[None], router_grad.T[None]


def solution(mesh):
    in_specs = (
        P("section", "ep", None),
        P("section", "ep", None),
        P("section", "ep", None),
        P("section", None, None, "ep"),
        P("section", None, None, "ep"),
        P("section", None, "ep"),
        P("section", None, "ep"),
        P("section", "ep", None),
    )
    out_specs = (P("section", "ep", None), P("section", "ep", None))
    return jax.shard_map(local, mesh=mesh, in_specs=in_specs, out_specs=out_specs, check_vma=False)
```

```python
import jax
import jax.numpy as jnp
from jax import lax
from jax.experimental import pallas as pl
from jax.experimental.pallas import tpu as pltpu
from jax.sharding import PartitionSpec as P

MESH = pl.DeviceIdType.MESH
BF = jnp.bfloat16
F32 = jnp.float32

SECTIONS = 8
E_WIN = 4
SLICES = 4
TOPK = 2
CAP = 80
TOK = 128
D = 7168
HID = 256
Q = D // SLICES
ROWS = SLICES * CAP
NQ = 7
QH = Q // NQ
FLY = 3

CW = 512
CA = 4096
NA = CA // CW
HA = NA // 2
HALF = CA // 2
WB = D - CA
NB = WB // CW
HB = NB // 2
HALFB = WB // 2
BLOCKS = (0, 1, 3, 2)


def dot_nt(a, b):
    return lax.dot_general(a, b, (((1,), (1,)), ((), ())), preferred_element_type=F32)


def place():
    s = lax.axis_index("section")
    p = lax.axis_index("ep")
    return s, p // SLICES, lax.rem(p, SLICES)


def shifted(a, by, n):
    return lax.rem(a + by + n, n)


def cols(start, width):
    return pl.ds(pl.multiple_of(start, 128), width)


def remote(src, dst, send, recv, device):
    return pltpu.make_async_remote_copy(
        src_ref=src, dst_ref=dst, send_sem=send, recv_sem=recv, device_id=device, device_id_type=MESH
    )


def layer_kernel(
    up, routes, gains, gate, upv, wg, wu, wd, out, router,
    info, slot_gain, pick, spread, gate_v, up_v, wdr, cot, parts, parts_sum, parts_in,
    grads, weights, partial, r1p, r1m, r2p, r2m, arecv, brecv, ctok, rb1p, rb1m, rb2p, rb2m,
    iz_s, iz_r, iy_s, iy_r, tok_s, tok_r, wd_s, wd_r, cot_s, cot_r, y_s, y_r,
    g1_s, g1_r, g2_s, g2_r, loc, out_s, pz_s, pz_r, py_s, py_r,
    w_sem, r1_s, r1_r, r2p_s, r2p_r, r2m_s, r2m_r, ay_s, ay_r, by_s, by_r, b1_s, b1_r, b2p_s, b2p_r, b2m_s, b2m_r,
):
    s, y, z = place()
    behind = shifted(s, -1, SECTIONS)
    ahead = shifted(s, 1, SECTIONS)
    zp, zm, z2 = shifted(z, 1, SLICES), shifted(z, -1, SLICES), shifted(z, 2, SLICES)

    def along_z(k):
        return (s, y * SLICES + shifted(z, k, SLICES))

    def along_y(k):
        return (s, shifted(y, k, E_WIN) * SLICES + z)

    right, left = along_z(1), along_z(3)

    barrier = pltpu.get_barrier_semaphore()
    for k in range(SLICES):
        pl.semaphore_signal(barrier, inc=1, device_id=(ahead, y * SLICES + k), device_id_type=MESH)
    for k in range(1, SLICES):
        pl.semaphore_signal(barrier, inc=1, device_id=along_z(k), device_id_type=MESH)
        pl.semaphore_signal(barrier, inc=1, device_id=along_y(k), device_id_type=MESH)

    def w_copy(c):
        take = pl.ds(c * CW, CW)
        return (
            pltpu.make_async_copy(wg.at[take], weights.at[c, :, pl.ds(0, HID)], w_sem.at[0, c]),
            pltpu.make_async_copy(wu.at[take], weights.at[c, :, pl.ds(HID, HID)], w_sem.at[1, c]),
        )

    wd_own = pltpu.make_async_copy(wd.at[:, cols(z * Q, Q)], wdr.at[z], loc.at[0])
    saved = (pltpu.make_async_copy(gate, gate_v, loc.at[1]), pltpu.make_async_copy(upv, up_v, loc.at[2]))

    info[y, z] = jnp.concatenate(
        [routes[...].astype(F32), gains[...].astype(F32), jnp.zeros((8 - 2 * TOPK, TOK), F32)], axis=0
    )
    parts[z] = jnp.zeros((E_WIN, 8, TOK), F32)
    row8 = lax.broadcasted_iota(jnp.int32, (8, TOK), 0).astype(F32)
    later = lax.broadcasted_iota(jnp.int32, (TOK, TOK), 1)
    earlier = lax.broadcasted_iota(jnp.int32, (TOK, TOK), 0)
    before = (earlier < later).astype(F32).astype(BF)
    unit = (earlier == later).astype(F32).astype(BF)
    slot_row = lax.broadcasted_iota(jnp.int32, (CAP, TOK), 0).astype(F32)
    lane_row = lax.broadcasted_iota(jnp.int32, (CAP, TOK), 1).astype(F32)

    pl.semaphore_wait(barrier, 10)

    def slots(e):
        return partial.at[e, :, :, pl.ds(0, Q)]

    def recv(owner):
        return partial.at[owner, :, :, pl.ds(Q, Q)]

    def back(n, yb):
        return partial.at[yb, :, :, pl.ds(2 * Q + n * HID, HID)]

    def ps(k, yb):
        return partial.at[yb, :, :, pl.ds(2 * Q + (2 + k) * HID, HID)]

    def g1(half, yb):
        return partial.at[yb, :, :, pl.ds(2 * Q + 6 * HID + half * (HID // 2), HID // 2)]

    def piece(ref, half):
        return ref.at[:, :, pl.ds(half * (HID // 2), HID // 2)]

    def tok(source, h):
        return ctok.at[source, :, cols(h * QH, QH)]

    def info_z(k, owner):
        return remote(info.at[y, z], info.at[y, owner], iz_s.at[k], iz_r.at[k], along_z(k))

    def info_y(k, owner):
        return remote(info.at[y], info.at[owner], iy_s.at[k], iy_r.at[k], along_y(k))

    def tok_copy(k, h, owner):
        q = shifted(z, k, SLICES)
        return remote(
            up.at[:, cols(q * Q + h * QH, QH)], tok(owner, h), tok_s.at[k, h], tok_r.at[k, h], (behind, y * SLICES + q)
        )

    def wd_copy(k, owner):
        q = shifted(z, k, SLICES)
        return remote(wd.at[:, cols(q * Q, Q)], wdr.at[owner], wd_s.at[k], wd_r.at[k], along_z(k))

    cot_copy = remote(up, cot, cot_s, cot_r, (behind, y * SLICES + z))

    def y_copy(k, h, owner):
        take = cols(h * QH, QH)
        return remote(
            slots(shifted(y, k, E_WIN)).at[:, :, take], recv(owner).at[:, :, take], y_s.at[k, h], y_r.at[k, h], along_y(k)
        )

    def g_first(half, m, yb):
        return remote(
            piece(ps(2, yb), half), g1(half, yb), g1_s.at[half, m], g1_r.at[half, m], (right, left)[half]
        )

    def g_second(side, half, m, yb):
        src = piece(ps((1, 3)[side], yb), half)
        return remote(
            src, piece(back(side, yb), half), g2_s.at[side, half, m], g2_r.at[side, half, m], (right, left)[side]
        )

    for k in (2, 1, 3):
        info_z(k, z).start()
    for h in range(FLY):
        for k in (2, 1, 3, 0):
            tok_copy(k, h, z).start()
    wd_own.start()
    for copy in saved:
        copy.start()

    def start_weights(c, _):
        for copy in w_copy(c):
            copy.start()
        return 0

    lax.fori_loop(0, D // CW, start_weights, 0)

    for k in (1, 3, 2):
        info_z(k, shifted(z, -k, SLICES)).wait_recv()
    for k in (2, 1, 3):
        info_y(k, y).start()

    def slot_of(block):
        hit = (block[0:1] == row8) | (block[1:2] == row8)
        rank = jnp.dot(hit.astype(F32).astype(BF), before, preferred_element_type=F32)
        return jnp.where(hit, rank, -1.0)

    def row_tables(zz, _):
        slot = slot_of(info[y, zz])
        for e in range(E_WIN):
            pick[zz, e] = (slot_row == slot[e:e + 1]).astype(F32).astype(BF)
        return 0

    lax.fori_loop(0, SLICES, row_tables, 0)

    def send_on(h):
        for k in range(SLICES):
            tok_copy(k, h, z).wait_send()
        for k in (2, 1, 3, 0):
            tok_copy(k, h + FLY, z).start()

    def pack(h):
        for k in (0, 1, 3, 2):
            tok_copy(k, h, shifted(z, -k, SLICES)).wait_recv()

        def pack_source(zz, _):
            rows = jnp.dot(pick[zz].reshape(E_WIN * CAP, TOK), tok(zz, h)[...], preferred_element_type=F32)
            partial[:, zz, :, cols(h * QH, QH)] = rows.astype(BF).reshape(E_WIN, CAP, QH)
            return 0

        lax.fori_loop(0, SLICES, pack_source, 0)
        for k in (1, 3, 2):
            y_copy(k, h, y).start()

    def dispatch(h, _):
        send_on(h)
        pack(h)
        return 0

    lax.fori_loop(0, NQ - FLY, dispatch, 0)
    for k in (2, 1, 3):
        wd_copy(k, z).start()
    cot_copy.start()

    def dispatch_rest(h, _):
        pack(h)
        return 0

    lax.fori_loop(NQ - FLY, NQ, dispatch_rest, 0)

    for k in (1, 3, 2):
        info_y(k, shifted(y, -k, E_WIN)).wait_recv()

    def expert_tables(i, _):
        b, zz = i // SLICES, lax.rem(i, SLICES)
        block = info[b, zz]
        here = y.astype(F32)
        slot = jnp.sum(jnp.where(row8 == here, slot_of(block), 0.0), axis=0, keepdims=True)
        gain = jnp.where(block[0:1] == here, block[2:3], 0.0) + jnp.where(block[1:2] == here, block[3:4], 0.0)
        slot_gain[b, zz, pl.ds(0, 1)] = slot
        slot_gain[b, zz, pl.ds(1, 1)] = gain
        return 0

    lax.fori_loop(0, E_WIN * SLICES, expert_tables, 0)

    def spread_tables(zz, _):
        spread[zz] = dot_nt(unit, pick[zz].reshape(E_WIN * CAP, TOK)).astype(BF)
        return 0

    lax.fori_loop(0, SLICES, spread_tables, 0)

    def block_of(m):
        return shifted(y, -m, E_WIN)

    def partial_grad(m):
        yb = block_of(m)
        if m:
            for h in range(NQ):
                y_copy(m, h, yb).wait_recv()

        def product(k):
            rows = (recv(yb) if m else slots(y))[...].reshape(ROWS, Q)
            return dot_nt(rows, wdr[shifted(z, k, SLICES)]).astype(BF).reshape(SLICES, CAP, HID)

        ps(2, yb)[...] = product(2)
        g_first(0, m, yb).start()
        g_first(1, m, yb).start()
        ps(1, yb)[...] = product(1)
        g_second(0, 1, m, yb).start()
        ps(3, yb)[...] = product(3)
        g_second(1, 0, m, yb).start()
        back(2, yb)[...] = product(0)

    def relay_grad(m):
        yb = block_of(m)
        for side in (0, 1):
            g_first(side, m, yb).wait_recv()
            mine = piece(ps((1, 3)[side], yb), side)
            mine[...] = (mine[...].astype(F32) + g1(side, yb)[...].astype(F32)).astype(BF)
            g_second(side, side, m, yb).start()

    def elementwise(m):
        yb = block_of(m)
        for side in (0, 1):
            for half in (0, 1):
                g_second(side, half, m, yb).wait_recv()

        def one(zz, _):
            total = back(0, yb)[zz].astype(F32) + back(1, yb)[zz].astype(F32) + back(2, yb)[zz].astype(F32)
            g = gate_v[yb * SLICES + zz].astype(F32)
            u = up_v[yb * SLICES + zz].astype(F32)
            held = slot_row == slot_gain[yb, zz, pl.ds(0, 1)]
            gain = jnp.sum(jnp.where(held, slot_gain[yb, zz, pl.ds(1, 1)], 0.0), axis=-1, keepdims=True)
            sig = 1.0 / (1.0 + jnp.exp(-g))
            silu = g * sig
            part = jnp.sum(silu * u * total, axis=-1, keepdims=True).astype(BF).astype(F32)
            parts[z, yb, pl.ds(zz, 1)] = jnp.sum(jnp.where(slot_row == lane_row, part, 0.0), axis=0, keepdims=True)
            scaled = total * gain
            grads[yb, zz, :, pl.ds(0, HID)] = (scaled * u * sig * (1.0 + g * (1.0 - sig))).astype(BF)
            grads[yb, zz, :, pl.ds(HID, HID)] = (scaled * silu).astype(BF)
            return 0

        lax.fori_loop(0, SLICES, one, 0)
        for half in (0, 1):
            g_first(half, m, yb).wait_send()
            for side in (0, 1):
                g_second(side, half, m, yb).wait_send()
        if m:
            for h in range(NQ):
                y_copy((E_WIN - m) % E_WIN, h, y).wait_send()

    def first(half, m, yb):
        src = partial.at[yb, z2, :, pl.ds(half * HALF, HALF)]
        return remote(src, (r1p, r1m)[half].at[yb], r1_s.at[half, m], r1_r.at[half, m], (right, left)[half])

    def to_right(half, m, yb):
        take = pl.ds(half * HALF, HALF)
        return remote(partial.at[yb, zp, :, take], r2p.at[yb, :, take], r2p_s.at[half, m], r2p_r.at[half, m], right)

    def to_left(half, m, yb):
        take = pl.ds(half * HALF, HALF)
        return remote(partial.at[yb, zm, :, take], r2m.at[yb, :, take], r2m_s.at[half, m], r2m_r.at[half, m], left)

    def a_copy(half, m, yb, owner):
        take = pl.ds(half * HALF, HALF)
        return remote(
            partial.at[yb, z, :, take], arecv.at[owner, :, take], ay_s.at[half, m], ay_r.at[half, m], along_y(-m)
        )

    def b_copy(half, m, yb, owner):
        return remote(
            partial.at[yb, :, :, pl.ds(CA + half * HALFB, HALFB)],
            brecv.at[:, owner, :, pl.ds(half * HALFB, HALFB)],
            by_s.at[half, m], by_r.at[half, m], along_y(-m),
        )

    def chunks_of(m, start, stop):
        yb = block_of(m)

        def chunk(c, _):
            part = dot_nt(grads[yb].reshape(ROWS, 2 * HID), weights[c])
            partial[yb, :, :, cols(c * CW, CW)] = part.astype(BF).reshape(SLICES, CAP, CW)
            return 0

        lax.fori_loop(start, stop, chunk, 0)
        return yb

    def input_a(m):
        yb = chunks_of(m, 0, HA)
        first(0, m, yb).start()
        to_left(0, m, yb).start()
        chunks_of(m, HA, NA)
        first(1, m, yb).start()
        to_right(1, m, yb).start()

    def input_b(m):
        for half in (0, 1):
            yb = chunks_of(m, NA + half * HB, NA + (half + 1) * HB)
            if m:
                b_copy(half, m, yb, y).start()
        if m == 0:

            def keep(zz, _):
                brecv[zz, y] = partial[y, zz, :, pl.ds(CA, WB)]
                return 0

            lax.fori_loop(0, SLICES, keep, 0)

    def relay(m):
        yb = block_of(m)
        for half in (0, 1):
            first(half, m, yb).wait_recv()

            def add(c, _):
                mine = partial.at[yb, (zp, zm)[half], :, cols(half * HALF + c * CW, CW)]
                other = (r1p, r1m)[half][yb, :, cols(c * CW, CW)]
                mine[...] = (mine[...].astype(F32) + other.astype(F32)).astype(BF)
                return 0

            lax.fori_loop(0, HA, add, 0)
            (to_right, to_left)[half](half, m, yb).start()

    def finish(m):
        yb = block_of(m)
        for half in (0, 1):
            to_right(half, m, yb).wait_recv()
            to_left(half, m, yb).wait_recv()

            def add(c, _):
                take = cols(half * HALF + c * CW, CW)
                mine = partial.at[yb, z, :, take]
                total = mine[...].astype(F32) + r2p[yb, :, take].astype(F32) + r2m[yb, :, take].astype(F32)
                if m:
                    mine[...] = total.astype(BF)
                else:
                    arecv[y, :, take] = total.astype(BF)
                return 0

            lax.fori_loop(0, HA, add, 0)
            if m:
                a_copy(half, m, yb, y).start()

    def parts_z(k, owner):
        return remote(parts.at[owner], parts.at[owner], pz_s.at[k], pz_r.at[k], along_z(k))

    def parts_y(m, owner):
        return remote(parts_sum.at[block_of(m)], parts_in.at[owner], py_s.at[m], py_r.at[m], along_y(-m))

    wd_own.wait()
    for k in (1, 3, 2):
        wd_copy(k, shifted(z, -k, SLICES)).wait_recv()
    for copy in saved:
        copy.wait()

    def weights_here(c, _):
        for copy in w_copy(c):
            copy.wait()
        return 0

    lax.fori_loop(0, D // CW, weights_here, 0)

    partial_grad(0)
    partial_grad(2)
    relay_grad(0)
    partial_grad(1)
    relay_grad(2)
    partial_grad(3)
    relay_grad(1)
    elementwise(0)
    relay_grad(3)
    input_a(0)
    for m in (2, 1, 3):
        elementwise(m)
        input_b(m)
    for k in (2, 1, 3):
        parts_z(k, z).start()
    input_a(1)
    relay(0)
    input_a(3)
    relay(1)
    input_a(2)
    relay(3)
    input_b(0)
    relay(2)

    for k in (1, 3, 2):
        parts_z(k, shifted(z, -k, SLICES)).wait_recv()
    parts_sum[...] = parts[0] + parts[1] + parts[2] + parts[3]
    for m in (1, 3, 2):
        parts_y(m, y).start()
    parts_in[y] = parts_sum[y]

    def b_first(half, j):
        src = ctok.at[z2, :, cols(j * CW, CW)]
        if half == 0:
            return remote(src, rb1p.at[:, cols(j * CW, CW)], b1_s.at[j], b1_r.at[j], right)
        return remote(src, rb1m.at[:, cols((j - HB) * CW, CW)], b1_s.at[j], b1_r.at[j], left)

    def b_right(j):
        return remote(ctok.at[zp, :, cols(j * CW, CW)], rb2p.at[:, cols(j * CW, CW)], b2p_s.at[j], b2p_r.at[j], right)

    def b_left(j):
        return remote(ctok.at[zm, :, cols(j * CW, CW)], rb2m.at[:, cols(j * CW, CW)], b2m_s.at[j], b2m_r.at[j], left)

    def tokens(half):
        for m in (1, 3, 2):
            b_copy(half, m, block_of(m), shifted(y, m, E_WIN)).wait_recv()

        def chunk(j, _):
            def combine(zz, _):
                rows = brecv[zz, :, :, cols(j * CW, CW)].reshape(E_WIN * CAP, CW)
                ctok[zz, :, cols(j * CW, CW)] = jnp.dot(spread[zz], rows, preferred_element_type=F32).astype(BF)
                return 0

            lax.fori_loop(0, SLICES, combine, 0)
            b_first(half, j).start()
            (b_left, b_right)[half](j).start()
            return 0

        lax.fori_loop(half * HB, (half + 1) * HB, chunk, 0)

    finish(0)
    finish(1)
    finish(3)
    finish(2)
    tokens(0)
    tokens(1)

    def relay_b(half, j):
        b_first(half, j).wait_recv()
        if half == 0:
            mine, other = ctok.at[zp, :, cols(j * CW, CW)], rb1p.at[:, cols(j * CW, CW)]
        else:
            mine, other = ctok.at[zm, :, cols(j * CW, CW)], rb1m.at[:, cols((j - HB) * CW, CW)]
        mine[...] = (mine[...].astype(F32) + other[...].astype(F32)).astype(BF)
        (b_right, b_left)[half](j).start()

    def relay_b_pair(i, _):
        relay_b(0, i)
        relay_b(1, HB + i)
        return 0

    lax.fori_loop(0, HB, relay_b_pair, 0)

    for m in (1, 3, 2):
        parts_y(m, shifted(y, m, E_WIN)).wait_recv()
    for k in range(TOPK):
        router[pl.ds(k, 1)] = jnp.zeros((1, TOK), F32)

    def router_part(e, _):
        row = parts_in[e, pl.ds(z, 1)]
        column = jnp.sum(jnp.where(slot_row == lane_row, row, 0.0), axis=-1, keepdims=True)
        values = jnp.sum(pick[z, e].astype(F32) * column, axis=0, keepdims=True)
        for k in range(TOPK):
            router[pl.ds(k, 1)] += jnp.where(routes[pl.ds(k, 1)] == e, values, 0.0)
        return 0

    lax.fori_loop(0, E_WIN, router_part, 0)

    def out_copy(c):
        return pltpu.make_async_copy(cot.at[:, cols(c * CW, CW)], out.at[:, cols(c * CW, CW)], out_s.at[c])

    cot_copy.wait_recv()
    for half in (0, 1):
        for m in (1, 3, 2):
            a_copy(half, m, block_of(m), shifted(y, m, E_WIN)).wait_recv()

        def last_a(c, _):
            take = cols(c * CW, CW)
            rows = arecv[:, :, take].reshape(E_WIN * CAP, CW)
            total = jnp.dot(spread[z], rows, preferred_element_type=F32)
            cot[:, take] = (cot[:, take].astype(F32) + total).astype(BF)
            out_copy(c).start()
            return 0

        lax.fori_loop(half * HA, (half + 1) * HA, last_a, 0)

    def last_b(j, _):
        b_right(j).wait_recv()
        b_left(j).wait_recv()
        take = cols(j * CW, CW)
        total = ctok[z, :, take].astype(F32) + rb2p[:, take].astype(F32) + rb2m[:, take].astype(F32)
        there = cols(CA + j * CW, CW)
        cot[:, there] = (cot[:, there].astype(F32) + total).astype(BF)
        out_copy(NA + j).start()
        return 0

    lax.fori_loop(0, NB, last_b, 0)

    def written(c, _):
        out_copy(c).wait()
        return 0

    lax.fori_loop(0, D // CW, written, 0)
    cot_copy.wait_send()
    for k in range(1, SLICES):
        info_z(k, z).wait_send()
        info_y(k, y).wait_send()
        wd_copy(k, z).wait_send()
        parts_z(k, z).wait_send()
        parts_y(k, y).wait_send()
    for h in range(NQ - FLY, NQ):
        for k in range(SLICES):
            tok_copy(k, h, z).wait_send()
    for half in (0, 1):
        for m in BLOCKS:
            yb = block_of(m)
            first(half, m, yb).wait_send()
            to_right(half, m, yb).wait_send()
            to_left(half, m, yb).wait_send()
            if m:
                a_copy(half, m, yb, y).wait_send()
                b_copy(half, m, yb, y).wait_send()

    def sent_b(half, j):
        b_first(half, j).wait_send()
        b_right(j).wait_send()
        b_left(j).wait_send()

    def sent_b_pair(i, _):
        sent_b(0, i)
        sent_b(1, HB + i)
        return 0

    lax.fori_loop(0, HB, sent_b_pair, 0)


def vmem(*shape, dtype=BF):
    return pltpu.VMEM(shape, dtype)


def sems(*shape):
    return pltpu.SemaphoreType.DMA(shape)


ANY = pl.BlockSpec(memory_space=pl.ANY)
VM = pl.BlockSpec(memory_space=pltpu.VMEM)


def layer(upstream, routes, gains, gate, up, w_gate, w_up, w_down):
    return pl.pallas_call(
        layer_kernel,
        out_shape=(
            jax.ShapeDtypeStruct((TOK, D), BF),
            jax.ShapeDtypeStruct((TOPK, TOK), F32),
        ),
        in_specs=[ANY, VM, VM, ANY, ANY, ANY, ANY, ANY],
        out_specs=(ANY, VM),
        scratch_shapes=[
            vmem(E_WIN, SLICES, 8, TOK, dtype=F32),
            vmem(E_WIN, SLICES, 8, TOK, dtype=F32),
            vmem(SLICES, E_WIN, CAP, TOK),
            vmem(SLICES, TOK, E_WIN * CAP),
            vmem(E_WIN * SLICES, CAP, HID),
            vmem(E_WIN * SLICES, CAP, HID),
            vmem(SLICES, HID, Q),
            vmem(TOK, D),
            vmem(SLICES, E_WIN, 8, TOK, dtype=F32),
            vmem(E_WIN, 8, TOK, dtype=F32),
            vmem(E_WIN, 8, TOK, dtype=F32),
            vmem(E_WIN, SLICES, CAP, 2 * HID),
            vmem(D // CW, CW, 2 * HID),
            vmem(E_WIN, SLICES, CAP, D),
            vmem(E_WIN, CAP, HALF),
            vmem(E_WIN, CAP, HALF),
            vmem(E_WIN, CAP, CA),
            vmem(E_WIN, CAP, CA),
            vmem(E_WIN, CAP, CA),
            vmem(SLICES, E_WIN, CAP, WB),
            vmem(SLICES, TOK, WB),
            vmem(TOK, HALFB),
            vmem(TOK, HALFB),
            vmem(TOK, WB),
            vmem(TOK, WB),
            sems(SLICES), sems(SLICES),
            sems(E_WIN), sems(E_WIN),
            sems(SLICES, NQ), sems(SLICES, NQ),
            sems(SLICES), sems(SLICES),
            pltpu.SemaphoreType.DMA, pltpu.SemaphoreType.DMA,
            sems(E_WIN, NQ), sems(E_WIN, NQ),
            sems(2, E_WIN), sems(2, E_WIN),
            sems(2, 2, E_WIN), sems(2, 2, E_WIN),
            sems(3),
            sems(D // CW),
            sems(SLICES), sems(SLICES),
            sems(E_WIN), sems(E_WIN),
            sems(2, D // CW),
            sems(2, E_WIN), sems(2, E_WIN),
            sems(2, E_WIN), sems(2, E_WIN),
            sems(2, E_WIN), sems(2, E_WIN),
            sems(2, E_WIN), sems(2, E_WIN),
            sems(2, E_WIN), sems(2, E_WIN),
            sems(NB), sems(NB),
            sems(NB), sems(NB),
            sems(NB), sems(NB),
        ],
        compiler_params=pltpu.CompilerParams(collective_id=0, has_side_effects=True, vmem_limit_bytes=63 * 2**20),
        name="layer",
    )(upstream, routes, gains, gate, up, w_gate, w_up, w_down)


def local(upstream, routes, combine_weights, gate_saved, up_saved, w_gate, w_up, w_down):
    grad_input, router_grad = layer(
        upstream[0], routes[0].T, combine_weights[0].T, gate_saved[0], up_saved[0], w_gate[0], w_up[0], w_down[0]
    )
    return grad_input[None], router_grad.T[None]


def solution(mesh):
    in_specs = (
        P("section", "ep", None),
        P("section", "ep", None),
        P("section", "ep", None),
        P("section", None, None, "ep"),
        P("section", None, None, "ep"),
        P("section", None, "ep"),
        P("section", None, "ep"),
        P("section", "ep", None),
    )
    out_specs = (P("section", "ep", None), P("section", "ep", None))
    return jax.shard_map(local, mesh=mesh, in_specs=in_specs, out_specs=out_specs, check_vma=False)
```

```python
import jax
import jax.numpy as jnp
from jax import lax
from jax.experimental import pallas as pl
from jax.experimental.pallas import tpu as pltpu
from jax.sharding import PartitionSpec as P

MESH = pl.DeviceIdType.MESH
BF = jnp.bfloat16
F32 = jnp.float32

SECTIONS = 8
E_WIN = 4
SLICES = 4
TOPK = 2
CAP = 80
TOK = 128
D = 7168
HID = 256
Q = D // SLICES
ROWS = SLICES * CAP
NQ = 7
QH = Q // NQ
FLY = 6

CA = 1024
WB = D - CA
CW = 512
FAR_W = D // 4
NEAR_W = CA // 2
BW = WB // 4
BC = BW // 2
BLOCKS = (0, 1, 3, 2)
NEAR = (0, 1, 3)
FAR_PIECES = [(2, n // 2, n * FAR_W, FAR_W, n) for n in range(4)]
NEAR_PIECES = [(m, n, n * NEAR_W, NEAR_W, 4 + 2 * NEAR.index(m) + n) for m in (1, 3, 0) for n in range(2)]
PIECES = FAR_PIECES + NEAR_PIECES


def dot_nt(a, b):
    return lax.dot_general(a, b, (((1,), (1,)), ((), ())), preferred_element_type=F32)


def place():
    s = lax.axis_index("section")
    p = lax.axis_index("ep")
    return s, p // SLICES, lax.rem(p, SLICES)


def shifted(a, by, n):
    return lax.rem(a + by + n, n)


def cols(start, width):
    return pl.ds(pl.multiple_of(start, 128), width)


def remote(src, dst, send, recv, device):
    return pltpu.make_async_remote_copy(
        src_ref=src, dst_ref=dst, send_sem=send, recv_sem=recv, device_id=device, device_id_type=MESH
    )


def layer_kernel(
    up, routes, gains, gate, upv, wg, wu, wd, out, router,
    info, slot_gain, pick, spread_near, spread_far, gate_v, up_v, wdr, cot, parts, parts_sum, parts_in,
    grads, weights, partial, r1f, r1n, r2pf, r2pn, r2mf, r2mn, af, an, brecv, ctok, rb1, rb2p, rb2m,
    iz_s, iz_r, iy_s, iy_r, tok_s, tok_r, wd_s, wd_r, cot_s, cot_r, y_s, y_r,
    g1_s, g1_r, g2_s, g2_r, loc, out_s, pz_s, pz_r, py_s, py_r,
    w_sem, r1_s, r1_r, r2p_s, r2p_r, r2m_s, r2m_r, ay_s, ay_r, by_s, by_r, b1_s, b1_r, b2p_s, b2p_r, b2m_s, b2m_r,
):
    s, y, z = place()
    behind = shifted(s, -1, SECTIONS)
    ahead = shifted(s, 1, SECTIONS)
    zp, zm, z2 = shifted(z, 1, SLICES), shifted(z, -1, SLICES), shifted(z, 2, SLICES)

    def along_z(k):
        return (s, y * SLICES + shifted(z, k, SLICES))

    def along_y(k):
        return (s, shifted(y, k, E_WIN) * SLICES + z)

    right, left = along_z(1), along_z(3)

    barrier = pltpu.get_barrier_semaphore()
    for k in range(SLICES):
        pl.semaphore_signal(barrier, inc=1, device_id=(ahead, y * SLICES + k), device_id_type=MESH)
    for k in range(1, SLICES):
        pl.semaphore_signal(barrier, inc=1, device_id=along_z(k), device_id_type=MESH)
        pl.semaphore_signal(barrier, inc=1, device_id=along_y(k), device_id_type=MESH)

    def w_copy(c):
        take = pl.ds(c * CW, CW)
        return (
            pltpu.make_async_copy(wg.at[take], weights.at[take, pl.ds(0, HID)], w_sem.at[0, c]),
            pltpu.make_async_copy(wu.at[take], weights.at[take, pl.ds(HID, HID)], w_sem.at[1, c]),
        )

    wd_own = pltpu.make_async_copy(wd.at[:, cols(z * Q, Q)], wdr.at[z], loc.at[0])
    saved = (pltpu.make_async_copy(gate, gate_v, loc.at[1]), pltpu.make_async_copy(upv, up_v, loc.at[2]))

    info[y, z] = jnp.concatenate(
        [routes[...].astype(F32), gains[...].astype(F32), jnp.zeros((8 - 2 * TOPK, TOK), F32)], axis=0
    )
    parts[z] = jnp.zeros((E_WIN, 8, TOK), F32)
    row8 = lax.broadcasted_iota(jnp.int32, (8, TOK), 0).astype(F32)
    later = lax.broadcasted_iota(jnp.int32, (TOK, TOK), 1)
    earlier = lax.broadcasted_iota(jnp.int32, (TOK, TOK), 0)
    before = (earlier < later).astype(F32).astype(BF)
    unit = (earlier == later).astype(F32).astype(BF)
    slot_row = lax.broadcasted_iota(jnp.int32, (CAP, TOK), 0).astype(F32)
    lane_row = lax.broadcasted_iota(jnp.int32, (CAP, TOK), 1).astype(F32)

    pl.semaphore_wait(barrier, 10)

    def slots(e):
        return partial.at[e, :, :, pl.ds(0, Q)]

    def recv(owner):
        return partial.at[owner, :, :, pl.ds(Q, Q)]

    def back(n, yb):
        return partial.at[yb, :, :, pl.ds(2 * Q + n * HID, HID)]

    def ps(k, yb):
        return partial.at[yb, :, :, pl.ds(2 * Q + (2 + k) * HID, HID)]

    def g1(half, yb):
        return partial.at[yb, :, :, pl.ds(2 * Q + 6 * HID + half * (HID // 2), HID // 2)]

    def piece(ref, half):
        return ref.at[:, :, pl.ds(half * (HID // 2), HID // 2)]

    def tok(source, h):
        return ctok.at[source, :, cols(h * QH, QH)]

    def info_z(k, owner):
        return remote(info.at[y, z], info.at[y, owner], iz_s.at[k], iz_r.at[k], along_z(k))

    def info_y(k, owner):
        return remote(info.at[y], info.at[owner], iy_s.at[k], iy_r.at[k], along_y(k))

    def tok_copy(k, h, owner):
        q = shifted(z, k, SLICES)
        return remote(
            up.at[:, cols(q * Q + h * QH, QH)], tok(owner, h), tok_s.at[k, h], tok_r.at[k, h], (behind, y * SLICES + q)
        )

    def wd_copy(k, owner):
        q = shifted(z, k, SLICES)
        return remote(wd.at[:, cols(q * Q, Q)], wdr.at[owner], wd_s.at[k], wd_r.at[k], along_z(k))

    cot_copy = remote(up, cot, cot_s, cot_r, (behind, y * SLICES + z))

    def y_copy(k, h, owner):
        take = cols(h * QH, QH)
        return remote(
            slots(shifted(y, k, E_WIN)).at[:, :, take], recv(owner).at[:, :, take], y_s.at[k, h], y_r.at[k, h], along_y(k)
        )

    def g_first(half, m, yb):
        return remote(
            piece(ps(2, yb), half), g1(half, yb), g1_s.at[half, m], g1_r.at[half, m], (right, left)[half]
        )

    def g_second(side, half, m, yb):
        src = piece(ps((1, 3)[side], yb), half)
        return remote(
            src, piece(back(side, yb), half), g2_s.at[side, half, m], g2_r.at[side, half, m], (right, left)[side]
        )

    for k in (2, 1, 3):
        info_z(k, z).start()
    for h in range(FLY):
        for k in (2, 1, 3, 0):
            tok_copy(k, h, z).start()
    wd_copy(2, z).start()
    wd_own.start()
    for copy in saved:
        copy.start()

    def start_weights(c, _):
        for copy in w_copy(c):
            copy.start()
        return 0

    lax.fori_loop(0, D // CW, start_weights, 0)

    for k in (1, 3, 2):
        info_z(k, shifted(z, -k, SLICES)).wait_recv()
    for k in (2, 1, 3):
        info_y(k, y).start()

    def slot_of(block):
        hit = (block[0:1] == row8) | (block[1:2] == row8)
        rank = jnp.dot(hit.astype(F32).astype(BF), before, preferred_element_type=F32)
        return jnp.where(hit, rank, -1.0)

    def row_tables(zz, _):
        slot = slot_of(info[y, zz])
        for e in range(E_WIN):
            pick[zz, e] = (slot_row == slot[e:e + 1]).astype(F32).astype(BF)
        return 0

    lax.fori_loop(0, SLICES, row_tables, 0)

    def send_on(h):
        for k in range(SLICES):
            tok_copy(k, h, z).wait_send()
        for k in (2, 1, 3, 0):
            tok_copy(k, h + FLY, z).start()

    def pack(h):
        for k in (0, 1, 3, 2):
            tok_copy(k, h, shifted(z, -k, SLICES)).wait_recv()

        def pack_source(zz, _):
            rows = jnp.dot(pick[zz].reshape(E_WIN * CAP, TOK), tok(zz, h)[...], preferred_element_type=F32)
            partial[:, zz, :, cols(h * QH, QH)] = rows.astype(BF).reshape(E_WIN, CAP, QH)
            return 0

        lax.fori_loop(0, SLICES, pack_source, 0)
        for k in (1, 3, 2):
            y_copy(k, h, y).start()

    def dispatch(h, _):
        send_on(h)
        pack(h)
        return 0

    lax.fori_loop(0, NQ - FLY, dispatch, 0)
    for k in (1, 3):
        wd_copy(k, z).start()
    cot_copy.start()

    def dispatch_rest(h, _):
        pack(h)
        return 0

    lax.fori_loop(NQ - FLY, NQ, dispatch_rest, 0)

    for k in (1, 3, 2):
        info_y(k, shifted(y, -k, E_WIN)).wait_recv()

    def expert_tables(i, _):
        b, zz = i // SLICES, lax.rem(i, SLICES)
        block = info[b, zz]
        here = y.astype(F32)
        slot = jnp.sum(jnp.where(row8 == here, slot_of(block), 0.0), axis=0, keepdims=True)
        gain = jnp.where(block[0:1] == here, block[2:3], 0.0) + jnp.where(block[1:2] == here, block[3:4], 0.0)
        slot_gain[b, zz, pl.ds(0, 1)] = slot
        slot_gain[b, zz, pl.ds(1, 1)] = gain
        return 0

    lax.fori_loop(0, E_WIN * SLICES, expert_tables, 0)

    def spread_tables(zz, _):
        rows = jnp.concatenate([pick[zz, shifted(y, m, E_WIN)] for m in NEAR], axis=0)
        spread_near[zz] = dot_nt(unit, rows).astype(BF)
        return 0

    lax.fori_loop(0, SLICES, spread_tables, 0)
    spread_far[...] = dot_nt(unit, pick[z, shifted(y, 2, E_WIN)]).astype(BF)

    def block_of(m):
        return shifted(y, -m, E_WIN)

    def partial_grad(m):
        yb = block_of(m)
        if m:
            for h in range(NQ):
                y_copy(m, h, yb).wait_recv()

        def product(k):
            rows = (recv(yb) if m else slots(y))[...].reshape(ROWS, Q)
            return dot_nt(rows, wdr[shifted(z, k, SLICES)]).astype(BF).reshape(SLICES, CAP, HID)

        ps(2, yb)[...] = product(2)
        g_first(0, m, yb).start()
        g_first(1, m, yb).start()
        ps(1, yb)[...] = product(1)
        g_second(0, 1, m, yb).start()
        ps(3, yb)[...] = product(3)
        g_second(1, 0, m, yb).start()
        back(2, yb)[...] = product(0)

    def relay_grad(m):
        yb = block_of(m)
        for side in (0, 1):
            g_first(side, m, yb).wait_recv()
            mine = piece(ps((1, 3)[side], yb), side)
            mine[...] = (mine[...].astype(F32) + g1(side, yb)[...].astype(F32)).astype(BF)
            g_second(side, side, m, yb).start()

    def elementwise(m):
        yb = block_of(m)
        for side in (0, 1):
            for half in (0, 1):
                g_second(side, half, m, yb).wait_recv()

        def one(zz, _):
            total = back(0, yb)[zz].astype(F32) + back(1, yb)[zz].astype(F32) + back(2, yb)[zz].astype(F32)
            g = gate_v[yb * SLICES + zz].astype(F32)
            u = up_v[yb * SLICES + zz].astype(F32)
            held = slot_row == slot_gain[yb, zz, pl.ds(0, 1)]
            gain = jnp.sum(jnp.where(held, slot_gain[yb, zz, pl.ds(1, 1)], 0.0), axis=-1, keepdims=True)
            sig = 1.0 / (1.0 + jnp.exp(-g))
            silu = g * sig
            part = jnp.sum(silu * u * total, axis=-1, keepdims=True).astype(BF).astype(F32)
            parts[z, yb, pl.ds(zz, 1)] = jnp.sum(jnp.where(slot_row == lane_row, part, 0.0), axis=0, keepdims=True)
            scaled = total * gain
            grads[yb, zz, :, pl.ds(0, HID)] = (scaled * u * sig * (1.0 + g * (1.0 - sig))).astype(BF)
            grads[yb, zz, :, pl.ds(HID, HID)] = (scaled * silu).astype(BF)
            return 0

        lax.fori_loop(0, SLICES, one, 0)
        for half in (0, 1):
            g_first(half, m, yb).wait_send()
            for side in (0, 1):
                g_second(side, half, m, yb).wait_send()
        if m:
            for h in range(NQ):
                y_copy((E_WIN - m) % E_WIN, h, y).wait_send()

    def there(far, near, piece):
        m, _, col, width, _ = piece
        if m == 2:
            return far.at[:, pl.ds(col, width)]
        return near.at[NEAR.index(m), :, pl.ds(col, width)]

    def mine(piece, zz):
        m, _, col, width, _ = piece
        return partial.at[block_of(m), zz, :, pl.ds(col, width)]

    def first(piece):
        half, i = piece[1], piece[4]
        return remote(mine(piece, z2), there(r1f, r1n, piece), r1_s.at[i], r1_r.at[i], (right, left)[half])

    def second(side, piece):
        i = piece[4]
        if side == 0:
            return remote(mine(piece, zp), there(r2pf, r2pn, piece), r2p_s.at[i], r2p_r.at[i], right)
        return remote(mine(piece, zm), there(r2mf, r2mn, piece), r2m_s.at[i], r2m_r.at[i], left)

    def a_copy(piece):
        m, i = piece[0], piece[4]
        return remote(mine(piece, z), there(af, an, piece), ay_s.at[i], ay_r.at[i], along_y(-m))

    def product(m, col, width, steps):
        yb = block_of(m)

        def chunk(c, _):
            take = cols(col + c * width, width)
            part = dot_nt(grads[yb].reshape(ROWS, 2 * HID), weights[pl.ds(pl.multiple_of(col + c * width, 128), width)])
            partial[yb, :, :, take] = part.astype(BF).reshape(SLICES, CAP, width)
            return 0

        lax.fori_loop(0, steps, chunk, 0)

    def produce(piece):
        m, half, col, width, _ = piece
        if m == 2:
            product(m, col, width // 2, 2)
        else:
            product(m, col, width, 1)
        first(piece).start()
        second(1 - half, piece).start()

    def relay(piece):
        half, width = piece[1], piece[3]
        first(piece).wait_recv()
        here, other = mine(piece, (zp, zm)[half]), there(r1f, r1n, piece)
        step = width // 2

        def add(c, _):
            take = cols(c * step, step)
            here[:, take] = (here[:, take].astype(F32) + other[:, take].astype(F32)).astype(BF)
            return 0

        lax.fori_loop(0, 2, add, 0)
        second(half, piece).start()

    def finish(piece):
        m, width = piece[0], piece[3]
        second(0, piece).wait_recv()
        second(1, piece).wait_recv()
        here, one, two = mine(piece, z), there(r2pf, r2pn, piece), there(r2mf, r2mn, piece)
        dest = here if m else there(af, an, piece)
        step = width // 2

        def add(c, _):
            take = cols(c * step, step)
            total = here[:, take].astype(F32) + one[:, take].astype(F32) + two[:, take].astype(F32)
            dest[:, take] = total.astype(BF)
            return 0

        lax.fori_loop(0, 2, add, 0)

    def b_copy(p, m):
        return remote(
            partial.at[block_of(m), :, :, pl.ds(CA + p * BW, BW)],
            brecv.at[:, NEAR.index(m), :, pl.ds(p * BW, BW)],
            by_s.at[p, m], by_r.at[p, m], along_y(-m),
        )

    def b_start(p):
        for m in (1, 3):
            b_copy(p, m).start()

    def b_sent(p):
        for m in (1, 3):
            b_copy(p, m).wait_send()

    def produce_b(p, m):
        product(m, CA + p * BW, BC, 2)
        if m == 0:

            def keep(zz, _):
                brecv[zz, 0, :, pl.ds(p * BW, BW)] = partial[y, zz, :, pl.ds(CA + p * BW, BW)]
                return 0

            lax.fori_loop(0, SLICES, keep, 0)

    def parts_z(k, owner):
        return remote(parts.at[owner], parts.at[owner], pz_s.at[k], pz_r.at[k], along_z(k))

    def parts_y(m, owner):
        return remote(parts_sum.at[block_of(m)], parts_in.at[owner], py_s.at[m], py_r.at[m], along_y(-m))

    wd_own.wait()
    for k in (1, 3, 2):
        wd_copy(k, shifted(z, -k, SLICES)).wait_recv()
    for copy in saved:
        copy.wait()

    def weights_here(c, _):
        for copy in w_copy(c):
            copy.wait()
        return 0

    lax.fori_loop(0, D // CW, weights_here, 0)

    def b_first(p):
        take = pl.ds(p * BW, BW)
        return remote(ctok.at[z2, :, take], rb1.at[:, take], b1_s.at[p], b1_r.at[p], (right, left)[p // 2])

    def b_second(side, p):
        take = pl.ds(p * BW, BW)
        if side == 0:
            return remote(ctok.at[zp, :, take], rb2p.at[:, take], b2p_s.at[p], b2p_r.at[p], right)
        return remote(ctok.at[zm, :, take], rb2m.at[:, take], b2m_s.at[p], b2m_r.at[p], left)

    def tokens(p):
        for m in (1, 3):
            b_copy(p, m).wait_recv()

        def combine(i, _):
            zz, take = i // 2, cols(p * BW + lax.rem(i, 2) * BC, BC)
            rows = brecv[zz, :, :, take].reshape(len(NEAR) * CAP, BC)
            ctok[zz, :, take] = jnp.dot(spread_near[zz], rows, preferred_element_type=F32).astype(BF)
            return 0

        lax.fori_loop(0, 2 * SLICES, combine, 0)
        b_first(p).start()
        b_second(1 - p // 2, p).start()

    def relay_b(p):
        b_first(p).wait_recv()

        def add(c, _):
            take = cols(p * BW + c * BC, BC)
            here = ctok.at[(zp, zm)[p // 2], :, take]
            here[...] = (here[...].astype(F32) + rb1[:, take].astype(F32)).astype(BF)
            return 0

        lax.fori_loop(0, 2, add, 0)
        b_second(p // 2, p).start()

    partial_grad(1)
    partial_grad(3)
    relay_grad(1)
    partial_grad(2)
    relay_grad(3)
    elementwise(1)
    relay_grad(2)
    partial_grad(0)
    elementwise(3)
    produce_b(0, 1)
    produce_b(0, 3)
    b_start(0)
    relay_grad(0)
    elementwise(2)
    produce(FAR_PIECES[0])
    produce(FAR_PIECES[2])
    produce_b(2, 1)
    produce_b(2, 3)
    b_start(2)
    produce(FAR_PIECES[1])
    produce(FAR_PIECES[3])
    elementwise(0)
    for k in (2, 1, 3):
        parts_z(k, z).start()
    for piece in NEAR_PIECES:
        produce(piece)
    for p in (1, 3):
        for m in (1, 3):
            produce_b(p, m)
    relay(FAR_PIECES[0])
    relay(FAR_PIECES[2])
    for p in range(4):
        produce_b(p, 0)
    relay(FAR_PIECES[1])
    relay(FAR_PIECES[3])
    for piece in NEAR_PIECES:
        relay(piece)

    for k in (1, 3, 2):
        parts_z(k, shifted(z, -k, SLICES)).wait_recv()
    parts_sum[...] = parts[0] + parts[1] + parts[2] + parts[3]
    for m in (1, 3, 2):
        parts_y(m, y).start()
    parts_in[y] = parts_sum[y]

    b_sent(0)
    b_start(1)
    b_sent(2)
    b_start(3)
    tokens(0)
    tokens(2)
    for n in (0, 2, 1, 3):
        finish(FAR_PIECES[n])
    relay_b(0)
    relay_b(2)
    b_sent(1)
    b_sent(3)
    for n in (0, 2, 1, 3):
        a_copy(FAR_PIECES[n]).start()
    tokens(1)
    tokens(3)
    for piece in NEAR_PIECES:
        finish(piece)
        if piece[0]:
            a_copy(piece).start()
    relay_b(1)
    relay_b(3)

    for m in (1, 3, 2):
        parts_y(m, shifted(y, m, E_WIN)).wait_recv()
    for k in range(TOPK):
        router[pl.ds(k, 1)] = jnp.zeros((1, TOK), F32)

    def router_part(e, _):
        row = parts_in[e, pl.ds(z, 1)]
        column = jnp.sum(jnp.where(slot_row == lane_row, row, 0.0), axis=-1, keepdims=True)
        values = jnp.sum(pick[z, e].astype(F32) * column, axis=0, keepdims=True)
        for k in range(TOPK):
            router[pl.ds(k, 1)] += jnp.where(routes[pl.ds(k, 1)] == e, values, 0.0)
        return 0

    lax.fori_loop(0, E_WIN, router_part, 0)

    def out_copy(c):
        return pltpu.make_async_copy(cot.at[:, cols(c * CW, CW)], out.at[:, cols(c * CW, CW)], out_s.at[c])

    cot_copy.wait_recv()
    for piece in PIECES:
        if piece[0]:
            a_copy(piece).wait_recv()

    def far_rows(take):
        return cot[:, take].astype(F32) + jnp.dot(spread_far[...], af[:, take], preferred_element_type=F32)

    def last_a(c, _):
        take = cols(c * CW, CW)
        rows = an[:, :, take].reshape(len(NEAR) * CAP, CW)
        total = jnp.dot(spread_near[z], rows, preferred_element_type=F32)
        cot[:, take] = (far_rows(take) + total).astype(BF)
        out_copy(c).start()
        return 0

    lax.fori_loop(0, CA // CW, last_a, 0)

    for p in (0, 2, 1, 3):
        b_second(0, p).wait_recv()
        b_second(1, p).wait_recv()

        def last_b(c, _):
            here = cols(p * BW + c * CW, CW)
            take = cols(CA + p * BW + c * CW, CW)
            total = ctok[z, :, here].astype(F32) + rb2p[:, here].astype(F32) + rb2m[:, here].astype(F32)
            cot[:, take] = (far_rows(take) + total).astype(BF)
            out_copy((CA + p * BW) // CW + c).start()
            return 0

        lax.fori_loop(0, BW // CW, last_b, 0)

    def written(c, _):
        out_copy(c).wait()
        return 0

    lax.fori_loop(0, D // CW, written, 0)
    cot_copy.wait_send()
    for k in range(1, SLICES):
        info_z(k, z).wait_send()
        info_y(k, y).wait_send()
        wd_copy(k, z).wait_send()
        parts_z(k, z).wait_send()
        parts_y(k, y).wait_send()
    for h in range(NQ - FLY, NQ):
        for k in range(SLICES):
            tok_copy(k, h, z).wait_send()
    for piece in PIECES:
        first(piece).wait_send()
        second(0, piece).wait_send()
        second(1, piece).wait_send()
        if piece[0]:
            a_copy(piece).wait_send()
    for p in range(4):
        b_first(p).wait_send()
        b_second(0, p).wait_send()
        b_second(1, p).wait_send()


def vmem(*shape, dtype=BF):
    return pltpu.VMEM(shape, dtype)


def sems(*shape):
    return pltpu.SemaphoreType.DMA(shape)


ANY = pl.BlockSpec(memory_space=pl.ANY)
VM = pl.BlockSpec(memory_space=pltpu.VMEM)


def layer(upstream, routes, gains, gate, up, w_gate, w_up, w_down):
    return pl.pallas_call(
        layer_kernel,
        out_shape=(
            jax.ShapeDtypeStruct((TOK, D), BF),
            jax.ShapeDtypeStruct((TOPK, TOK), F32),
        ),
        in_specs=[ANY, VM, VM, ANY, ANY, ANY, ANY, ANY],
        out_specs=(ANY, VM),
        scratch_shapes=[
            vmem(E_WIN, SLICES, 8, TOK, dtype=F32),
            vmem(E_WIN, SLICES, 8, TOK, dtype=F32),
            vmem(SLICES, E_WIN, CAP, TOK),
            vmem(SLICES, TOK, len(NEAR) * CAP),
            vmem(TOK, CAP),
            vmem(E_WIN * SLICES, CAP, HID),
            vmem(E_WIN * SLICES, CAP, HID),
            vmem(SLICES, HID, Q),
            vmem(TOK, D),
            vmem(SLICES, E_WIN, 8, TOK, dtype=F32),
            vmem(E_WIN, 8, TOK, dtype=F32),
            vmem(E_WIN, 8, TOK, dtype=F32),
            vmem(E_WIN, SLICES, CAP, 2 * HID),
            vmem(D, 2 * HID),
            vmem(E_WIN, SLICES, CAP, D),
            vmem(CAP, D), vmem(len(NEAR), CAP, CA),
            vmem(CAP, D), vmem(len(NEAR), CAP, CA),
            vmem(CAP, D), vmem(len(NEAR), CAP, CA),
            vmem(CAP, D), vmem(len(NEAR), CAP, CA),
            vmem(SLICES, len(NEAR), CAP, WB),
            vmem(SLICES, TOK, WB),
            vmem(TOK, WB),
            vmem(TOK, WB),
            vmem(TOK, WB),
            sems(SLICES), sems(SLICES),
            sems(E_WIN), sems(E_WIN),
            sems(SLICES, NQ), sems(SLICES, NQ),
            sems(SLICES), sems(SLICES),
            pltpu.SemaphoreType.DMA, pltpu.SemaphoreType.DMA,
            sems(E_WIN, NQ), sems(E_WIN, NQ),
            sems(2, E_WIN), sems(2, E_WIN),
            sems(2, 2, E_WIN), sems(2, 2, E_WIN),
            sems(3),
            sems(D // CW),
            sems(SLICES), sems(SLICES),
            sems(E_WIN), sems(E_WIN),
            sems(2, D // CW),
            sems(len(PIECES)), sems(len(PIECES)),
            sems(len(PIECES)), sems(len(PIECES)),
            sems(len(PIECES)), sems(len(PIECES)),
            sems(len(PIECES)), sems(len(PIECES)),
            sems(4, E_WIN), sems(4, E_WIN),
            sems(4), sems(4),
            sems(4), sems(4),
            sems(4), sems(4),
        ],
        compiler_params=pltpu.CompilerParams(collective_id=0, has_side_effects=True, vmem_limit_bytes=63 * 2**20),
        name="layer",
    )(upstream, routes, gains, gate, up, w_gate, w_up, w_down)


def local(upstream, routes, combine_weights, gate_saved, up_saved, w_gate, w_up, w_down):
    grad_input, router_grad = layer(
        upstream[0], routes[0].T, combine_weights[0].T, gate_saved[0], up_saved[0], w_gate[0], w_up[0], w_down[0]
    )
    return grad_input[None], router_grad.T[None]


def solution(mesh):
    in_specs = (
        P("section", "ep", None),
        P("section", "ep", None),
        P("section", "ep", None),
        P("section", None, None, "ep"),
        P("section", None, None, "ep"),
        P("section", None, "ep"),
        P("section", None, "ep"),
        P("section", "ep", None),
    )
    out_specs = (P("section", "ep", None), P("section", "ep", None))
    return jax.shard_map(local, mesh=mesh, in_specs=in_specs, out_specs=out_specs, check_vma=False)
```

```python
import jax
import jax.numpy as jnp
from jax import lax
from jax.experimental import pallas as pl
from jax.experimental.pallas import tpu as pltpu
from jax.sharding import PartitionSpec as P

MESH = pl.DeviceIdType.MESH
BF = jnp.bfloat16
F32 = jnp.float32

SECTIONS = 8
E_WIN = 4
SLICES = 4
TOPK = 2
CAP = 80
TOK = 128
D = 7168
HID = 256
Q = D // SLICES
ROWS = SLICES * CAP
NQ = 7
QH = Q // NQ
FLY = 6

CA = 1024
WB = D - CA
CW = 512
FAR_W = D // 4
NEAR_W = CA // 2
BW = WB // 4
BC = BW // 2
BLOCKS = (0, 1, 3, 2)
NEAR = (0, 1, 3)
FAR_PIECES = [(2, n // 2, n * FAR_W, FAR_W, n) for n in range(4)]
NEAR_PIECES = [(m, n, n * NEAR_W, NEAR_W, 4 + 2 * NEAR.index(m) + n) for m in (1, 3, 0) for n in range(2)]
PIECES = FAR_PIECES + NEAR_PIECES


def dot_nt(a, b):
    return lax.dot_general(a, b, (((1,), (1,)), ((), ())), preferred_element_type=F32)


def place():
    s = lax.axis_index("section")
    p = lax.axis_index("ep")
    return s, p // SLICES, lax.rem(p, SLICES)


def shifted(a, by, n):
    return lax.rem(a + by + n, n)


def cols(start, width):
    return pl.ds(pl.multiple_of(start, 128), width)


def remote(src, dst, send, recv, device):
    return pltpu.make_async_remote_copy(
        src_ref=src, dst_ref=dst, send_sem=send, recv_sem=recv, device_id=device, device_id_type=MESH
    )


def layer_kernel(
    up, routes, gains, gate, upv, wg, wu, wd, out, router,
    info, slot_gain, pick, spread_near, spread_far, gate_v, up_v, wdr, cot, parts, parts_sum, parts_in,
    grads, weights, partial, r1f, r1n, r2pf, r2pn, r2mf, r2mn, af, an, brecv, ctok, rb1, rb2p, rb2m,
    iz_s, iz_r, iy_s, iy_r, tok_s, tok_r, wd_s, wd_r, cot_s, cot_r, y_s, y_r,
    g1_s, g1_r, g2_s, g2_r, loc, out_s, pz_s, pz_r, py_s, py_r,
    w_sem, r1_s, r1_r, r2p_s, r2p_r, r2m_s, r2m_r, ay_s, ay_r, by_s, by_r, b1_s, b1_r, b2p_s, b2p_r, b2m_s, b2m_r,
):
    s, y, z = place()
    behind = shifted(s, -1, SECTIONS)
    ahead = shifted(s, 1, SECTIONS)
    zp, zm, z2 = shifted(z, 1, SLICES), shifted(z, -1, SLICES), shifted(z, 2, SLICES)

    def along_z(k):
        return (s, y * SLICES + shifted(z, k, SLICES))

    def along_y(k):
        return (s, shifted(y, k, E_WIN) * SLICES + z)

    right, left = along_z(1), along_z(3)

    barrier = pltpu.get_barrier_semaphore()
    for k in range(SLICES):
        pl.semaphore_signal(barrier, inc=1, device_id=(ahead, y * SLICES + k), device_id_type=MESH)
    for k in range(1, SLICES):
        pl.semaphore_signal(barrier, inc=1, device_id=along_z(k), device_id_type=MESH)
        pl.semaphore_signal(barrier, inc=1, device_id=along_y(k), device_id_type=MESH)

    def w_copy(c):
        take = pl.ds(c * CW, CW)
        return (
            pltpu.make_async_copy(wg.at[take], weights.at[take, pl.ds(0, HID)], w_sem.at[0, c]),
            pltpu.make_async_copy(wu.at[take], weights.at[take, pl.ds(HID, HID)], w_sem.at[1, c]),
        )

    wd_own = pltpu.make_async_copy(wd.at[:, cols(z * Q, Q)], wdr.at[z], loc.at[0])
    saved = (pltpu.make_async_copy(gate, gate_v, loc.at[1]), pltpu.make_async_copy(upv, up_v, loc.at[2]))

    info[y, z] = jnp.concatenate(
        [routes[...].astype(F32), gains[...].astype(F32), jnp.zeros((8 - 2 * TOPK, TOK), F32)], axis=0
    )
    parts[z] = jnp.zeros((E_WIN, 8, TOK), F32)
    row8 = lax.broadcasted_iota(jnp.int32, (8, TOK), 0).astype(F32)
    later = lax.broadcasted_iota(jnp.int32, (TOK, TOK), 1)
    earlier = lax.broadcasted_iota(jnp.int32, (TOK, TOK), 0)
    before = (earlier < later).astype(F32).astype(BF)
    unit = (earlier == later).astype(F32).astype(BF)
    slot_row = lax.broadcasted_iota(jnp.int32, (CAP, TOK), 0).astype(F32)
    lane_row = lax.broadcasted_iota(jnp.int32, (CAP, TOK), 1).astype(F32)

    pl.semaphore_wait(barrier, 10)

    def slots(e):
        return partial.at[e, :, :, pl.ds(0, Q)]

    def recv(owner):
        return partial.at[owner, :, :, pl.ds(Q, Q)]

    def back(n, yb):
        return partial.at[yb, :, :, pl.ds(2 * Q + n * HID, HID)]

    def ps(k, yb):
        return partial.at[yb, :, :, pl.ds(2 * Q + (2 + k) * HID, HID)]

    def g1(half, yb):
        return partial.at[yb, :, :, pl.ds(2 * Q + 6 * HID + half * (HID // 2), HID // 2)]

    def piece(ref, half):
        return ref.at[:, :, pl.ds(half * (HID // 2), HID // 2)]

    def tok(source, h):
        return ctok.at[source, :, cols(h * QH, QH)]

    def info_z(k, owner):
        return remote(info.at[y, z], info.at[y, owner], iz_s.at[k], iz_r.at[k], along_z(k))

    def info_y(k, owner):
        return remote(info.at[y], info.at[owner], iy_s.at[k], iy_r.at[k], along_y(k))

    def tok_copy(k, h, owner):
        q = shifted(z, k, SLICES)
        return remote(
            up.at[:, cols(q * Q + h * QH, QH)], tok(owner, h), tok_s.at[k, h], tok_r.at[k, h], (behind, y * SLICES + q)
        )

    def wd_copy(k, owner):
        q = shifted(z, k, SLICES)
        return remote(wd.at[:, cols(q * Q, Q)], wdr.at[owner], wd_s.at[k], wd_r.at[k], along_z(k))

    cot_copy = remote(up, cot, cot_s, cot_r, (behind, y * SLICES + z))

    def y_copy(k, h, owner):
        take = cols(h * QH, QH)
        return remote(
            slots(shifted(y, k, E_WIN)).at[:, :, take], recv(owner).at[:, :, take], y_s.at[k, h], y_r.at[k, h], along_y(k)
        )

    def g_first(half, m, yb):
        return remote(
            piece(ps(2, yb), half), g1(half, yb), g1_s.at[half, m], g1_r.at[half, m], (right, left)[half]
        )

    def g_second(side, half, m, yb):
        src = piece(ps((1, 3)[side], yb), half)
        return remote(
            src, piece(back(side, yb), half), g2_s.at[side, half, m], g2_r.at[side, half, m], (right, left)[side]
        )

    for k in (2, 1, 3):
        info_z(k, z).start()
    for h in range(FLY):
        for k in (2, 1, 3, 0):
            tok_copy(k, h, z).start()
    wd_copy(2, z).start()
    wd_own.start()
    for copy in saved:
        copy.start()

    def start_weights(c, _):
        for copy in w_copy(c):
            copy.start()
        return 0

    lax.fori_loop(0, D // CW, start_weights, 0)

    for k in (1, 3, 2):
        info_z(k, shifted(z, -k, SLICES)).wait_recv()
    for k in (2, 1, 3):
        info_y(k, y).start()

    def slot_of(block):
        hit = (block[0:1] == row8) | (block[1:2] == row8)
        rank = jnp.dot(hit.astype(F32).astype(BF), before, preferred_element_type=F32)
        return jnp.where(hit, rank, -1.0)

    def row_tables(zz, _):
        slot = slot_of(info[y, zz])
        for e in range(E_WIN):
            pick[zz, e] = (slot_row == slot[e:e + 1]).astype(F32).astype(BF)
        return 0

    lax.fori_loop(0, SLICES, row_tables, 0)

    def send_on(h):
        for k in range(SLICES):
            tok_copy(k, h, z).wait_send()
        for k in (2, 1, 3, 0):
            tok_copy(k, h + FLY, z).start()

    def pack(h):
        for k in (0, 1, 3, 2):
            tok_copy(k, h, shifted(z, -k, SLICES)).wait_recv()

        def pack_source(zz, _):
            rows = jnp.dot(pick[zz].reshape(E_WIN * CAP, TOK), tok(zz, h)[...], preferred_element_type=F32)
            partial[:, zz, :, cols(h * QH, QH)] = rows.astype(BF).reshape(E_WIN, CAP, QH)
            return 0

        lax.fori_loop(0, SLICES, pack_source, 0)
        for k in (1, 3, 2):
            y_copy(k, h, y).start()

    def dispatch(h, _):
        send_on(h)
        pack(h)
        return 0

    lax.fori_loop(0, NQ - FLY, dispatch, 0)
    for k in (1, 3):
        wd_copy(k, z).start()
    cot_copy.start()

    def dispatch_rest(h, _):
        pack(h)
        return 0

    lax.fori_loop(NQ - FLY, NQ, dispatch_rest, 0)

    for k in (1, 3, 2):
        info_y(k, shifted(y, -k, E_WIN)).wait_recv()

    def expert_tables(i, _):
        b, zz = i // SLICES, lax.rem(i, SLICES)
        block = info[b, zz]
        here = y.astype(F32)
        slot = jnp.sum(jnp.where(row8 == here, slot_of(block), 0.0), axis=0, keepdims=True)
        gain = jnp.where(block[0:1] == here, block[2:3], 0.0) + jnp.where(block[1:2] == here, block[3:4], 0.0)
        slot_gain[b, zz, pl.ds(0, 1)] = slot
        slot_gain[b, zz, pl.ds(1, 1)] = gain
        return 0

    lax.fori_loop(0, E_WIN * SLICES, expert_tables, 0)

    def spread_tables(zz, _):
        rows = jnp.concatenate([pick[zz, shifted(y, m, E_WIN)] for m in NEAR], axis=0)
        spread_near[zz] = dot_nt(unit, rows).astype(BF)
        return 0

    lax.fori_loop(0, SLICES, spread_tables, 0)
    spread_far[...] = dot_nt(unit, pick[z, shifted(y, 2, E_WIN)]).astype(BF)

    def block_of(m):
        return shifted(y, -m, E_WIN)

    def partial_grad(m):
        yb = block_of(m)
        if m:
            for h in range(NQ):
                y_copy(m, h, yb).wait_recv()

        def product(k):
            rows = (recv(yb) if m else slots(y))[...].reshape(ROWS, Q)
            return dot_nt(rows, wdr[shifted(z, k, SLICES)]).astype(BF).reshape(SLICES, CAP, HID)

        ps(2, yb)[...] = product(2)
        g_first(0, m, yb).start()
        g_first(1, m, yb).start()
        ps(1, yb)[...] = product(1)
        g_second(0, 1, m, yb).start()
        ps(3, yb)[...] = product(3)
        g_second(1, 0, m, yb).start()
        back(2, yb)[...] = product(0)

    def relay_grad(m):
        yb = block_of(m)
        for side in (0, 1):
            g_first(side, m, yb).wait_recv()
            mine = piece(ps((1, 3)[side], yb), side)
            mine[...] = (mine[...].astype(F32) + g1(side, yb)[...].astype(F32)).astype(BF)
            g_second(side, side, m, yb).start()

    def elementwise(m):
        yb = block_of(m)
        for side in (0, 1):
            for half in (0, 1):
                g_second(side, half, m, yb).wait_recv()

        def one(zz, _):
            total = back(0, yb)[zz].astype(F32) + back(1, yb)[zz].astype(F32) + back(2, yb)[zz].astype(F32)
            g = gate_v[yb * SLICES + zz].astype(F32)
            u = up_v[yb * SLICES + zz].astype(F32)
            held = slot_row == slot_gain[yb, zz, pl.ds(0, 1)]
            gain = jnp.sum(jnp.where(held, slot_gain[yb, zz, pl.ds(1, 1)], 0.0), axis=-1, keepdims=True)
            sig = 1.0 / (1.0 + jnp.exp(-g))
            silu = g * sig
            part = jnp.sum(silu * u * total, axis=-1, keepdims=True).astype(BF).astype(F32)
            parts[z, yb, pl.ds(zz, 1)] = jnp.sum(jnp.where(slot_row == lane_row, part, 0.0), axis=0, keepdims=True)
            scaled = total * gain
            grads[yb, zz, :, pl.ds(0, HID)] = (scaled * u * sig * (1.0 + g * (1.0 - sig))).astype(BF)
            grads[yb, zz, :, pl.ds(HID, HID)] = (scaled * silu).astype(BF)
            return 0

        lax.fori_loop(0, SLICES, one, 0)
        for half in (0, 1):
            g_first(half, m, yb).wait_send()
            for side in (0, 1):
                g_second(side, half, m, yb).wait_send()
        if m:
            for h in range(NQ):
                y_copy((E_WIN - m) % E_WIN, h, y).wait_send()

    def there(far, near, piece):
        m, _, col, width, _ = piece
        if m == 2:
            return far.at[:, pl.ds(col, width)]
        return near.at[NEAR.index(m), :, pl.ds(col, width)]

    def mine(piece, zz):
        m, _, col, width, _ = piece
        return partial.at[block_of(m), zz, :, pl.ds(col, width)]

    def first(piece):
        half, i = piece[1], piece[4]
        return remote(mine(piece, z2), there(r1f, r1n, piece), r1_s.at[i], r1_r.at[i], (right, left)[half])

    def second(side, piece):
        i = piece[4]
        if side == 0:
            return remote(mine(piece, zp), there(r2pf, r2pn, piece), r2p_s.at[i], r2p_r.at[i], right)
        return remote(mine(piece, zm), there(r2mf, r2mn, piece), r2m_s.at[i], r2m_r.at[i], left)

    def a_copy(piece):
        m, i = piece[0], piece[4]
        return remote(mine(piece, z), there(af, an, piece), ay_s.at[i], ay_r.at[i], along_y(-m))

    def product(m, col, width, steps):
        yb = block_of(m)

        def chunk(c, _):
            take = cols(col + c * width, width)
            part = dot_nt(grads[yb].reshape(ROWS, 2 * HID), weights[pl.ds(pl.multiple_of(col + c * width, 128), width)])
            partial[yb, :, :, take] = part.astype(BF).reshape(SLICES, CAP, width)
            return 0

        lax.fori_loop(0, steps, chunk, 0)

    def produce(piece):
        m, half, col, width, _ = piece
        if m == 2:
            product(m, col, width // 2, 2)
        else:
            product(m, col, width, 1)
        first(piece).start()
        second(1 - half, piece).start()

    def relay(piece):
        half, width = piece[1], piece[3]
        first(piece).wait_recv()
        here, other = mine(piece, (zp, zm)[half]), there(r1f, r1n, piece)
        step = width // 2

        def add(c, _):
            take = cols(c * step, step)
            here[:, take] = (here[:, take].astype(F32) + other[:, take].astype(F32)).astype(BF)
            return 0

        lax.fori_loop(0, 2, add, 0)
        second(half, piece).start()

    def finish(piece):
        m, width = piece[0], piece[3]
        second(0, piece).wait_recv()
        second(1, piece).wait_recv()
        here, one, two = mine(piece, z), there(r2pf, r2pn, piece), there(r2mf, r2mn, piece)
        dest = here if m else there(af, an, piece)
        step = width // 2

        def add(c, _):
            take = cols(c * step, step)
            total = here[:, take].astype(F32) + one[:, take].astype(F32) + two[:, take].astype(F32)
            dest[:, take] = total.astype(BF)
            return 0

        lax.fori_loop(0, 2, add, 0)

    def b_copy(p, m):
        return remote(
            partial.at[block_of(m), :, :, pl.ds(CA + p * BW, BW)],
            brecv.at[:, NEAR.index(m), :, pl.ds(p * BW, BW)],
            by_s.at[p, m], by_r.at[p, m], along_y(-m),
        )

    def b_start(p):
        for m in (1, 3):
            b_copy(p, m).start()

    def b_sent(p):
        for m in (1, 3):
            b_copy(p, m).wait_send()

    def produce_b(p, m):
        product(m, CA + p * BW, BC, 2)
        if m == 0:

            def keep(zz, _):
                brecv[zz, 0, :, pl.ds(p * BW, BW)] = partial[y, zz, :, pl.ds(CA + p * BW, BW)]
                return 0

            lax.fori_loop(0, SLICES, keep, 0)

    def parts_z(k, owner):
        return remote(parts.at[owner], parts.at[owner], pz_s.at[k], pz_r.at[k], along_z(k))

    def parts_y(m, owner):
        return remote(parts_sum.at[block_of(m)], parts_in.at[owner], py_s.at[m], py_r.at[m], along_y(-m))

    wd_own.wait()
    for k in (1, 3, 2):
        wd_copy(k, shifted(z, -k, SLICES)).wait_recv()
    for copy in saved:
        copy.wait()

    def weights_here(c, _):
        for copy in w_copy(c):
            copy.wait()
        return 0

    lax.fori_loop(0, D // CW, weights_here, 0)

    def b_first(p):
        take = pl.ds(p * BW, BW)
        return remote(ctok.at[z2, :, take], rb1.at[:, take], b1_s.at[p], b1_r.at[p], (right, left)[p // 2])

    def b_second(side, p):
        take = pl.ds(p * BW, BW)
        if side == 0:
            return remote(ctok.at[zp, :, take], rb2p.at[:, take], b2p_s.at[p], b2p_r.at[p], right)
        return remote(ctok.at[zm, :, take], rb2m.at[:, take], b2m_s.at[p], b2m_r.at[p], left)

    def tokens(p):
        for m in (1, 3):
            b_copy(p, m).wait_recv()

        def combine(i, _):
            zz, take = i // 2, cols(p * BW + lax.rem(i, 2) * BC, BC)
            rows = brecv[zz, :, :, take].reshape(len(NEAR) * CAP, BC)
            ctok[zz, :, take] = jnp.dot(spread_near[zz], rows, preferred_element_type=F32).astype(BF)
            return 0

        lax.fori_loop(0, 2 * SLICES, combine, 0)
        b_first(p).start()
        b_second(1 - p // 2, p).start()

    def relay_b(p):
        b_first(p).wait_recv()

        def add(c, _):
            take = cols(p * BW + c * BC, BC)
            here = ctok.at[(zp, zm)[p // 2], :, take]
            here[...] = (here[...].astype(F32) + rb1[:, take].astype(F32)).astype(BF)
            return 0

        lax.fori_loop(0, 2, add, 0)
        b_second(p // 2, p).start()

    partial_grad(1)
    partial_grad(3)
    relay_grad(1)
    partial_grad(2)
    relay_grad(3)
    elementwise(1)
    relay_grad(2)
    partial_grad(0)
    elementwise(3)
    produce_b(0, 1)
    produce_b(0, 3)
    b_start(0)
    relay_grad(0)
    elementwise(2)
    produce(FAR_PIECES[0])
    produce(FAR_PIECES[2])
    produce_b(2, 1)
    produce_b(2, 3)
    b_start(2)
    produce(FAR_PIECES[1])
    produce(FAR_PIECES[3])
    elementwise(0)
    for k in (2, 1, 3):
        parts_z(k, z).start()
    for piece in NEAR_PIECES:
        produce(piece)
    for p in (1, 3):
        for m in (1, 3):
            produce_b(p, m)
    relay(FAR_PIECES[0])
    relay(FAR_PIECES[2])
    for p in range(4):
        produce_b(p, 0)
    relay(FAR_PIECES[1])
    relay(FAR_PIECES[3])
    for piece in NEAR_PIECES:
        relay(piece)

    for k in (1, 3, 2):
        parts_z(k, shifted(z, -k, SLICES)).wait_recv()
    parts_sum[...] = parts[0] + parts[1] + parts[2] + parts[3]
    for m in (1, 3, 2):
        parts_y(m, y).start()
    parts_in[y] = parts_sum[y]

    b_sent(0)
    b_start(1)
    b_sent(2)
    b_start(3)
    tokens(0)
    tokens(2)
    for n in (0, 2, 1, 3):
        finish(FAR_PIECES[n])
    relay_b(0)
    relay_b(2)
    b_sent(1)
    b_sent(3)
    for n in (0, 2, 1, 3):
        a_copy(FAR_PIECES[n]).start()
    tokens(1)
    tokens(3)
    for piece in NEAR_PIECES:
        finish(piece)
        if piece[0]:
            a_copy(piece).start()
    relay_b(1)
    relay_b(3)

    for m in (1, 3, 2):
        parts_y(m, shifted(y, m, E_WIN)).wait_recv()
    for k in range(TOPK):
        router[pl.ds(k, 1)] = jnp.zeros((1, TOK), F32)

    def router_part(e, _):
        row = parts_in[e, pl.ds(z, 1)]
        column = jnp.sum(jnp.where(slot_row == lane_row, row, 0.0), axis=-1, keepdims=True)
        values = jnp.sum(pick[z, e].astype(F32) * column, axis=0, keepdims=True)
        for k in range(TOPK):
            router[pl.ds(k, 1)] += jnp.where(routes[pl.ds(k, 1)] == e, values, 0.0)
        return 0

    lax.fori_loop(0, E_WIN, router_part, 0)

    def out_copy(c):
        return pltpu.make_async_copy(cot.at[:, cols(c * CW, CW)], out.at[:, cols(c * CW, CW)], out_s.at[c])

    cot_copy.wait_recv()
    def far_rows(take):
        return cot[:, take].astype(F32) + jnp.dot(spread_far[...], af[:, take], preferred_element_type=F32)

    def last_a(c, _):
        take = cols(c * CW, CW)
        rows = an[:, :, take].reshape(len(NEAR) * CAP, CW)
        total = jnp.dot(spread_near[z], rows, preferred_element_type=F32)
        cot[:, take] = (far_rows(take) + total).astype(BF)
        out_copy(c).start()
        return 0

    for p in (0, 2, 1, 3):
        for n in {0: (0, 1), 2: (2, 3)}.get(p, ()):
            a_copy(FAR_PIECES[n]).wait_recv()
        if p == 1:
            for piece in NEAR_PIECES:
                if piece[0]:
                    a_copy(piece).wait_recv()
            lax.fori_loop(0, CA // CW, last_a, 0)
        b_second(0, p).wait_recv()
        b_second(1, p).wait_recv()

        def last_b(c, _):
            here = cols(p * BW + c * CW, CW)
            take = cols(CA + p * BW + c * CW, CW)
            total = ctok[z, :, here].astype(F32) + rb2p[:, here].astype(F32) + rb2m[:, here].astype(F32)
            cot[:, take] = (far_rows(take) + total).astype(BF)
            out_copy((CA + p * BW) // CW + c).start()
            return 0

        lax.fori_loop(0, BW // CW, last_b, 0)

    def written(c, _):
        out_copy(c).wait()
        return 0

    lax.fori_loop(0, D // CW, written, 0)
    cot_copy.wait_send()
    for k in range(1, SLICES):
        info_z(k, z).wait_send()
        info_y(k, y).wait_send()
        wd_copy(k, z).wait_send()
        parts_z(k, z).wait_send()
        parts_y(k, y).wait_send()
    for h in range(NQ - FLY, NQ):
        for k in range(SLICES):
            tok_copy(k, h, z).wait_send()
    for piece in PIECES:
        first(piece).wait_send()
        second(0, piece).wait_send()
        second(1, piece).wait_send()
        if piece[0]:
            a_copy(piece).wait_send()
    for p in range(4):
        b_first(p).wait_send()
        b_second(0, p).wait_send()
        b_second(1, p).wait_send()


def vmem(*shape, dtype=BF):
    return pltpu.VMEM(shape, dtype)


def sems(*shape):
    return pltpu.SemaphoreType.DMA(shape)


ANY = pl.BlockSpec(memory_space=pl.ANY)
VM = pl.BlockSpec(memory_space=pltpu.VMEM)


def layer(upstream, routes, gains, gate, up, w_gate, w_up, w_down):
    return pl.pallas_call(
        layer_kernel,
        out_shape=(
            jax.ShapeDtypeStruct((TOK, D), BF),
            jax.ShapeDtypeStruct((TOPK, TOK), F32),
        ),
        in_specs=[ANY, VM, VM, ANY, ANY, ANY, ANY, ANY],
        out_specs=(ANY, VM),
        scratch_shapes=[
            vmem(E_WIN, SLICES, 8, TOK, dtype=F32),
            vmem(E_WIN, SLICES, 8, TOK, dtype=F32),
            vmem(SLICES, E_WIN, CAP, TOK),
            vmem(SLICES, TOK, len(NEAR) * CAP),
            vmem(TOK, CAP),
            vmem(E_WIN * SLICES, CAP, HID),
            vmem(E_WIN * SLICES, CAP, HID),
            vmem(SLICES, HID, Q),
            vmem(TOK, D),
            vmem(SLICES, E_WIN, 8, TOK, dtype=F32),
            vmem(E_WIN, 8, TOK, dtype=F32),
            vmem(E_WIN, 8, TOK, dtype=F32),
            vmem(E_WIN, SLICES, CAP, 2 * HID),
            vmem(D, 2 * HID),
            vmem(E_WIN, SLICES, CAP, D),
            vmem(CAP, D), vmem(len(NEAR), CAP, CA),
            vmem(CAP, D), vmem(len(NEAR), CAP, CA),
            vmem(CAP, D), vmem(len(NEAR), CAP, CA),
            vmem(CAP, D), vmem(len(NEAR), CAP, CA),
            vmem(SLICES, len(NEAR), CAP, WB),
            vmem(SLICES, TOK, WB),
            vmem(TOK, WB),
            vmem(TOK, WB),
            vmem(TOK, WB),
            sems(SLICES), sems(SLICES),
            sems(E_WIN), sems(E_WIN),
            sems(SLICES, NQ), sems(SLICES, NQ),
            sems(SLICES), sems(SLICES),
            pltpu.SemaphoreType.DMA, pltpu.SemaphoreType.DMA,
            sems(E_WIN, NQ), sems(E_WIN, NQ),
            sems(2, E_WIN), sems(2, E_WIN),
            sems(2, 2, E_WIN), sems(2, 2, E_WIN),
            sems(3),
            sems(D // CW),
            sems(SLICES), sems(SLICES),
            sems(E_WIN), sems(E_WIN),
            sems(2, D // CW),
            sems(len(PIECES)), sems(len(PIECES)),
            sems(len(PIECES)), sems(len(PIECES)),
            sems(len(PIECES)), sems(len(PIECES)),
            sems(len(PIECES)), sems(len(PIECES)),
            sems(4, E_WIN), sems(4, E_WIN),
            sems(4), sems(4),
            sems(4), sems(4),
            sems(4), sems(4),
        ],
        compiler_params=pltpu.CompilerParams(collective_id=0, has_side_effects=True, vmem_limit_bytes=63 * 2**20),
        name="layer",
    )(upstream, routes, gains, gate, up, w_gate, w_up, w_down)


def local(upstream, routes, combine_weights, gate_saved, up_saved, w_gate, w_up, w_down):
    grad_input, router_grad = layer(
        upstream[0], routes[0].T, combine_weights[0].T, gate_saved[0], up_saved[0], w_gate[0], w_up[0], w_down[0]
    )
    return grad_input[None], router_grad.T[None]


def solution(mesh):
    in_specs = (
        P("section", "ep", None),
        P("section", "ep", None),
        P("section", "ep", None),
        P("section", None, None, "ep"),
        P("section", None, None, "ep"),
        P("section", None, "ep"),
        P("section", None, "ep"),
        P("section", "ep", None),
    )
    out_specs = (P("section", "ep", None), P("section", "ep", None))
    return jax.shard_map(local, mesh=mesh, in_specs=in_specs, out_specs=out_specs, check_vma=False)
```
